32 devices in a mesh: dp: 8 (over z, x), tensor: 4 (over y, core).
Axes of the slice: x: 2, y: 2, z: 4, core: 2. Of those that a mesh axis runs over, the one named last changes fastest.
Arguments:
- images: bfloat16 [24, 729, 1152], P('dp', None, 'tensor'), may hold values from -6 to 6
- image_count: int32 [8], P('dp'), may hold values from 2 to 3, as said below
- attn_gain: float32 [1152], replicated, may hold values from 0.5 to 1.5
- attn_shift: float32 [1152], replicated, may hold values from -1.8 to 1.8
- query_weight: bfloat16 [1152, 1152], P('dp', 'tensor'), may hold values from -0.25 to 0.25
- query_bias: float32 [1152], P('tensor'), may hold values from -3 to 3
- key_weight: bfloat16 [1152, 1152], P('dp', 'tensor'), may hold values from -0.25 to 0.25
- value_weight: bfloat16 [1152, 1152], P('dp', 'tensor'), may hold values from -0.1875 to 0.1875
- value_bias: float32 [1152], P('tensor'), may hold values from -3 to 3
- output_weight: bfloat16 [1152, 1152], P('tensor', 'dp'), may hold values from -1 to 1
- output_bias: float32 [1152], P('tensor'), may hold values from -3 to 3
- mlp_gain: float32 [1152], replicated, may hold values from 0.5 to 1.5
- mlp_shift: float32 [1152], replicated, may hold values from -1.8 to 1.8
- up_weight: bfloat16 [1152, 4304], P('dp', 'tensor'), may hold values from -0.1875 to 0.1875
- up_bias: float32 [4304], P('tensor'), may hold values from -3 to 3
- down_weight: bfloat16 [4304, 1152], P('tensor', 'dp'), may hold values from -0.125 to 0.125
- down_bias: float32 [1152], P('tensor'), may hold values from -3 to 3
- cotangent: bfloat16 [24, 729, 1152], P('dp', None, 'tensor'), may hold values from -6 to 6
Outputs:
- layer_out: bfloat16 [24, 729, 1152], P('dp', None, 'tensor')
- image_grad: bfloat16 [24, 729, 1152], P('dp', None, 'tensor')
- attn_gain_grad: float32 [1152], P('tensor')
- attn_shift_grad: float32 [1152], P('tensor')
- query_weight_grad: float32 [1152, 1152], P('dp', 'tensor')
- query_bias_grad: float32 [1152], P('tensor')
- key_weight_grad: float32 [1152, 1152], P('dp', 'tensor')
- value_weight_grad: float32 [1152, 1152], P('dp', 'tensor')
- value_bias_grad: float32 [1152], P('tensor')
- output_weight_grad: float32 [1152, 1152], P('tensor', 'dp')
- output_bias_grad: float32 [1152], P('tensor')
- mlp_gain_grad: float32 [1152], P('tensor')
- mlp_shift_grad: float32 [1152], P('tensor')
- up_weight_grad: float32 [1152, 4304], P('dp', 'tensor')
- up_bias_grad: float32 [4304], P('tensor')
- down_weight_grad: float32 [4304, 1152], P('tensor', 'dp')
- down_bias_grad: float32 [1152], P('tensor')
The draws below stay inside these ranges and needn't reach their ends.
Inputs may be any that keep to these rules, and one draw needn't show every extreme that they name: Slots 0 to image_count - 1 of a data position hold its images; some position has 3 images and some has 2.
All inputs are finite; a program needn't handle non-finite values.
Results may differ from the reference program's by a relative error of at most 0.017.
Values may be sent and summed in bfloat16 or wider, within the bound.
No kernel may reach another device: no remote copies, remote signals or barrier semaphores. Data moves between devices by JAX's collectives and lax.ppermute only.
A program may use at most 256 MiB of HBM per device.

```python
import math
import jax
import jax.numpy as jnp
from jax import lax

HEADS = 16
HDIM = 72
D = 1152
FF = 4304
SEQ = 729
MB = 3
SLOTS = 24
N_DP = 8


def draw_image_count(key, part):
    key = jax.random.fold_in(key, 7)
    count_key, order_key = jax.random.split(key)
    counts = jax.random.randint(count_key, (N_DP,), MB - 1, MB + 1).astype(jnp.int32)
    ranking = jax.random.permutation(order_key, N_DP)
    counts = counts.at[ranking[0]].set(MB).at[ranking[1]].set(MB - 1)
    return counts


def shard_levels(rng, shape, shards, low, high):
    factor_of = 1.0
    for axis_at, parts in shards:
        steps = jax.random.uniform(jax.random.fold_in(jax.random.fold_in(rng, 6), axis_at), (parts,), jnp.float32, low / len(shards), high / len(shards))
        factor_of = factor_of * jnp.repeat(jnp.exp(steps), shape[axis_at] // parts).reshape((-1,) + (1,) * (len(shape) - 1 - axis_at))
    return factor_of


def normal_values(rng, dims, deviation, limit, cuts=(), kind=jnp.bfloat16):
    entries = jax.random.normal(rng, dims, jnp.float32) * deviation
    if len(cuts) > 0:
        entries = shard_levels(rng, dims, cuts, -0.22, 0.18) * entries
    return jnp.clip(entries, min=-limit, max=limit).astype(kind)


def setup_inputs(seed: int = 0) -> dict:
    key_of = jax.random.split(jax.random.key(seed), 19)
    return {
        "images": normal_values(key_of[0], (SLOTS, SEQ, D), 1.0, 6.0, ((0, 8), (2, 4))),
        "image_count": draw_image_count(jax.random.fold_in(key_of[18], 71), 0),
        "attn_gain": jnp.clip(1.0 + 0.1 * jax.random.normal(key_of[2], (D,), jnp.float32), 0.5, 1.5),
        "attn_shift": normal_values(key_of[3], (D,), 0.3, 1.8, (), jnp.float32),
        "query_weight": normal_values(key_of[4], (D, D), (D // 2) ** -0.5, 0.25, ((0, 8), (1, 4))),
        "query_bias": normal_values(key_of[5], (D,), 0.5, 3.0, ((0, 4),), jnp.float32),
        "key_weight": normal_values(key_of[6], (D, D), (D // 2) ** -0.5, 0.25, ((0, 8), (1, 4))),
        "value_weight": normal_values(key_of[7], (D, D), D ** -0.5, 0.1875, ((0, 8), (1, 4))),
        "value_bias": normal_values(key_of[8], (D,), 0.5, 3.0, ((0, 4),), jnp.float32),
        "output_weight": normal_values(key_of[9], (D, D), (D // 32) ** -0.5, 1.0, ((0, 4), (1, 8))),
        "output_bias": normal_values(key_of[10], (D,), 0.5, 3.0, ((0, 4),), jnp.float32),
        "mlp_gain": jnp.clip(1.0 + 0.1 * jax.random.normal(key_of[11], (D,), jnp.float32), 0.5, 1.5),
        "mlp_shift": normal_values(key_of[12], (D,), 0.3, 1.8, (), jnp.float32),
        "up_weight": normal_values(key_of[13], (D, FF), D ** -0.5, 0.1875, ((0, 8), (1, 4))),
        "up_bias": normal_values(key_of[14], (FF,), 0.5, 3.0, ((0, 4),), jnp.float32),
        "down_weight": normal_values(key_of[15], (FF, D), (FF // 2) ** -0.5, 0.125, ((0, 4), (1, 8))),
        "down_bias": normal_values(key_of[16], (D,), 0.5, 3.0, ((0, 4),), jnp.float32),
        "cotangent": normal_values(key_of[17], (SLOTS, SEQ, D), 1.0, 6.0, ((0, 8), (2, 4))),
    }


@jax.custom_vjp
def low(v):
    return lax.optimization_barrier(v.astype(jnp.bfloat16)).astype(jnp.float32)

@jax.custom_vjp
def low_back(v):
    return v

def low_keep(v):
    return (low(v), None)

def low_pass(kept, grad):
    return (grad,)

def back_keep(v):
    return (v, None)

def back_low(kept, grad):
    return (low(grad),)
low.defvjp(low_keep, low_pass)
low_back.defvjp(back_keep, back_low)

def normalize(rows):
    centred = rows - lax.optimization_barrier(jnp.mean(rows, axis=1, keepdims=True))
    inverse = lax.rsqrt(lax.optimization_barrier(jnp.mean(centred * centred, axis=1, keepdims=True)) + 1e-06)
    return centred * inverse

def gelu_tanh(value):
    return jax.nn.gelu(value, approximate=True)

def image_layer(params, rows):
    attn_gain, attn_shift, query_weight, query_bias, key_weight, value_weight, value_bias, output_weight, output_bias, mlp_gain, mlp_shift, up_weight, up_bias, down_weight, down_bias = params
    highest = lax.Precision.HIGHEST
    attn_in = low(normalize(rows) * attn_gain + attn_shift)
    query = low(low_back(jnp.dot(attn_in, query_weight, precision=highest) + query_bias))
    keys_all = low(low_back(jnp.dot(attn_in, key_weight, precision=highest)))
    values_all = low(low_back(jnp.dot(attn_in, value_weight, precision=highest) + value_bias))
    query_heads = query.reshape(SEQ, HEADS, HDIM).transpose(1, 0, 2)
    key_heads = keys_all.reshape(SEQ, HEADS, HDIM).transpose(1, 0, 2)
    value_heads = values_all.reshape(SEQ, HEADS, HDIM).transpose(1, 0, 2)
    scores = low_back(jnp.einsum('hqd,hkd->hqk', query_heads, key_heads, precision=highest) * (1.0 / math.sqrt(HDIM)))
    shifted = scores - lax.optimization_barrier(jnp.max(scores, axis=-1, keepdims=True))
    weights_exp = jnp.exp(shifted)
    probs = low(weights_exp / lax.optimization_barrier(jnp.sum(weights_exp, axis=-1, keepdims=True)))
    mixed_heads = jnp.einsum('hqk,hkd->hqd', probs, value_heads, precision=highest)
    mixed = low(low_back(mixed_heads.transpose(1, 0, 2).reshape(SEQ, HEADS * HDIM)))
    hidden1 = rows + low_back(jnp.dot(mixed, output_weight, precision=highest)) + output_bias
    mlp_in = low(normalize(hidden1) * mlp_gain + mlp_shift)
    pre_act = low_back(jnp.dot(mlp_in, up_weight, precision=highest) + up_bias)
    activ = low(gelu_tanh(pre_act))
    return hidden1 + low_back(jnp.dot(activ, down_weight, precision=highest)) + down_bias

def forward(images, params, live_flags):
    step_fn = jax.checkpoint(lambda rows: image_layer(params, rows))

    def scan_step(carry, rows):
        return (carry, step_fn(rows))
    unused, results = lax.scan(scan_step, jnp.zeros((), jnp.float32), images)
    return results * live_flags[:, None, None]

def reference(images, image_count, attn_gain, attn_shift, query_weight, query_bias, key_weight, value_weight, value_bias, output_weight, output_bias, mlp_gain, mlp_shift, up_weight, up_bias, down_weight, down_bias, cotangent):
    params = tuple((item.astype(jnp.float32) for item in (attn_gain, attn_shift, query_weight, query_bias, key_weight, value_weight, value_bias, output_weight, output_bias, mlp_gain, mlp_shift, up_weight, up_bias, down_weight, down_bias)))
    slot_ids = jnp.arange(MB, dtype=jnp.int32)
    live_flags = (slot_ids[None, :] < image_count[:, None]).reshape(-1).astype(jnp.float32)
    result, pullback = jax.vjp(lambda rows, weights: forward(rows, weights, live_flags), images.astype(jnp.float32), params)
    input_grad, grads = pullback(cotangent.astype(jnp.float32))
    return (result.astype(jnp.bfloat16), input_grad.astype(jnp.bfloat16), grads[0], grads[1], grads[2], grads[3], grads[4], grads[5], grads[6], grads[7], grads[8], grads[9], grads[10], grads[11], grads[12], grads[13], grads[14])
```

```python
import functools
import math

import jax
import jax.numpy as jnp
from jax import lax
from jax.experimental import pallas as pl
from jax.experimental.pallas import tpu as pltpu
from jax.sharding import PartitionSpec as P

HDIM = 72
EPSILON = 1e-06
LOG2E = 1.4426950408889634
MASKED = -1e30
GELU_A = math.sqrt(2.0 / math.pi)
GELU_B = 0.044715
TILE = 256
VMEM_LIMIT = 56 * 2**20
F32 = jnp.float32
LOW = jnp.bfloat16
Y_SWAP = [(0, 2), (2, 0), (1, 3), (3, 1)]
CORE_SWAP = [(0, 1), (1, 0), (2, 3), (3, 2)]


def y_swap(value):
    return lax.ppermute(value, "tensor", Y_SWAP)


def core_swap(value):
    return lax.ppermute(value, "tensor", CORE_SWAP)


def dot_nn(a, b):
    return lax.dot_general(a, b, (((1,), (0,)), ((), ())), preferred_element_type=F32)


def dot_nt(a, b):
    return lax.dot_general(a, b, (((1,), (1,)), ((), ())), preferred_element_type=F32)


def dot_tn(a, b):
    return lax.dot_general(a, b, (((0,), (0,)), ((), ())), preferred_element_type=F32)


def rel_blocks(value, t):
    width = value.shape[0] // 4
    return jnp.concatenate(
        [lax.dynamic_slice_in_dim(value, (t ^ m) * width, width, 0) for m in (0, 2, 1, 3)], axis=0
    )


def rows4(a, b, c, d):
    return jnp.concatenate([a, b, c, d], axis=0)


def lanes(count):
    return [slice(at, at + TILE) for at in range(0, count, TILE)]


def column(sums):
    pad = jnp.zeros((sums[0].shape[0], 8 - len(sums)), F32)
    return jnp.concatenate([*sums, pad], axis=1)


def prepare_kernel(x, bias, out):
    slots, share, seq = x.shape
    high = bias[:, 0:1].astype(LOW)
    rest = bias[:, 0:1] - high.astype(F32)
    mid = rest.astype(LOW)
    for i in range(slots):
        out[i] = jnp.zeros(out.shape[1:], LOW)
        out[i, :, :seq] = x[i]
        out[i, :, seq : seq + 1] = high
        out[i, :, seq + 1 : seq + 2] = mid
        out[i, :, seq + 2 : seq + 3] = (rest - mid.astype(F32)).astype(LOW)


def prepare_grad_kernel(live, x, out, sums):
    slots, share, seq = x.shape
    total = 0.0
    for i in range(slots):
        out[i] = jnp.zeros(out.shape[1:], LOW)
        out[i, :, :seq] = (x[i].astype(F32) * live[i]).astype(LOW)
        total = total + dot_nt(jnp.ones((8, out.shape[2]), LOW), out[i])
    sums[...] = total


def place_kernel(pos, *refs):
    count = len(refs) - 3
    far, out, turned = refs[count:]
    for m in range(count):
        out[pos[2 * m]] = refs[m][...]
        out[pos[2 * m + 1]] = far[m]
    rows = out.shape[0] * out.shape[1]
    turned[...] = out[...].reshape(rows, out.shape[2]).T


def join_kernel(near, far, out, turned):
    rows, half = near.shape
    out[:, :half] = near[...]
    out[: rows // 2, half:] = far[rows // 2 :]
    out[rows // 2 :, half:] = far[: rows // 2]
    turned[...] = near[:, : half // 2].T


def attn_fwd_kernel(seq, xo, xy, xc, xd, vec, w, bias, attn_in, qkv, mixed, stats, lse):
    share, count = xo.shape
    heads = share // HDIM
    gain, shift = vec[:, 0:1], vec[:, 1:2]
    for at in lanes(count):
        x = rows4(xo[:, at], xy[:, at], xc[:, at], xd[:, at]).astype(F32)
        mean = jnp.mean(x, axis=0, keepdims=True)
        centred = x - mean
        inverse = lax.rsqrt(jnp.mean(centred * centred, axis=0, keepdims=True) + EPSILON)
        low = (centred * inverse * gain + shift).astype(LOW)
        attn_in[:, at] = low
        stats[0:1, at] = mean
        stats[1:2, at] = inverse
        part = dot_nn(w[...], low) + bias[:, 0:1]
        for i in range(3 * heads):
            qkv[i, :, at] = part[i * HDIM : (i + 1) * HDIM].astype(LOW)
    c = LOG2E / math.sqrt(HDIM)
    mask = lax.broadcasted_iota(jnp.int32, (count, 1), 0) < seq
    out = []
    for h in range(heads):
        q, k, v = qkv[h], qkv[heads + h], qkv[2 * heads + h]
        s = jnp.where(mask, dot_tn(k, q), MASKED)
        top = jnp.max(s, axis=0, keepdims=True)
        e = jnp.exp2((s - top) * c)
        total = jnp.sum(e, axis=0, keepdims=True)
        lse[h : h + 1, :] = top * c + jnp.log2(total)
        out.append(dot_nn(v, e.astype(LOW)) * (1.0 / total))
    mixed[...] = jnp.concatenate(out, axis=0).astype(LOW)


def mlp_fwd_kernel(
    seq, xo, xy, xc, xd, mo, my, mc, md, vec, w_out, up, up_bias, down,
    mlp_in, norm2, activ, slope, base, stats, keep, send,
):
    share, count = xo.shape
    gain, shift = vec[:, 3:4], vec[:, 4:5]
    tail = rows4(xo[:, seq:], xy[:, seq:], xc[:, seq:], xd[:, seq:]).astype(F32)
    o_bias = tail[:, 0:1] + tail[:, 1:2] + tail[:, 2:3]
    for at in lanes(count):
        mixed = rows4(mo[:, at], my[:, at], mc[:, at], md[:, at])
        x = rows4(xo[:, at], xy[:, at], xc[:, at], xd[:, at]).astype(F32)
        hidden = x + dot_nn(w_out[...], mixed) + o_bias
        mean = jnp.mean(hidden, axis=0, keepdims=True)
        centred = hidden - mean
        inverse = lax.rsqrt(jnp.mean(centred * centred, axis=0, keepdims=True) + EPSILON)
        normed = centred * inverse
        stats[0:1, at] = inverse
        norm2[:, at] = normed.astype(LOW)
        low = (normed * gain + shift).astype(LOW)
        mlp_in[:, at] = low
        v = dot_nn(up[...], low) + up_bias[:, 0:1]
        square = v * v
        tanh = jnp.tanh(v * (GELU_A + GELU_A * GELU_B * square))
        gate = 0.5 + 0.5 * tanh
        act = (v * gate).astype(LOW)
        activ[:, at] = act
        slope[:, at] = (
            gate + v * (0.5 - 0.5 * tanh * tanh) * (GELU_A + 3.0 * GELU_A * GELU_B * square)
        ).astype(LOW)
        part = dot_nn(down[...], act)
        base[:, at] = hidden[:share] + part[:share] + vec[:share, 5:6]
        keep[:, at] = part[share : 2 * share]
        send[0, :, at] = part[2 * share : 3 * share].astype(LOW)
        send[1, :, at] = part[3 * share :].astype(LOW)


def mlp_bwd_kernel(co, cy, cc, cd, slope, down, up, cot, pre_grad, keep, send, sums):
    share, count = co.shape
    for at in lanes(count):
        c = rows4(co[:, at], cy[:, at], cc[:, at], cd[:, at])
        cot[:, at] = c
        low = (dot_nn(down[...], c) * slope[:, at].astype(F32)).astype(LOW)
        pre_grad[:, at] = low
        part = dot_nn(up[...], low)
        keep[0, :, at] = part[:share]
        keep[1, :, at] = part[share : 2 * share]
        send[0, :, at] = part[2 * share : 3 * share].astype(LOW)
        send[1, :, at] = part[3 * share :].astype(LOW)
    sums[...] = dot_nt(jnp.ones((8, count), LOW), pre_grad[...])


def attn_bwd_kernel(
    seq, half, across, far, cot, norm2, stats2, vec, w_out, qkv, lse, w, attn_in,
    branch, h_grad, dqkv, keep_o, keep_y, send, stats, sums_own, sums_qkv,
    dmix,
):
    width, count = cot.shape
    share = width // 4
    heads = share // HDIM
    gain2 = vec[:, 3:4]
    sums = [0.0, 0.0, 0.0]
    for at in lanes(count):
        near = half[:, :, at] + across[:, :, at].astype(F32)
        ng = rows4(near[0], near[1], far[0, :, at].astype(F32), far[1, :, at].astype(F32))
        n2 = norm2[:, at].astype(F32)
        g = ng * gain2
        first = jnp.mean(g, axis=0, keepdims=True)
        second = jnp.mean(g * n2, axis=0, keepdims=True)
        hg = cot[:, at].astype(F32) + stats2[0:1, at] * (g - first - n2 * second)
        h_grad[:, at] = hg[:share]
        low = hg.astype(LOW)
        branch[:, at] = low
        dm = dot_nn(w_out[...], low)
        for h in range(heads):
            dmix[h, :, at] = dm[h * HDIM : (h + 1) * HDIM].astype(LOW)
        own = ng[:share]
        now = [hg[:share], own * n2[:share], own]
        sums = [a + jnp.sum(b, axis=1, keepdims=True) for a, b in zip(sums, now)]
    sums_own[...] = column(sums)
    scale = 1.0 / math.sqrt(HDIM)
    c = LOG2E * scale
    mask = lax.broadcasted_iota(jnp.int32, (count, 1), 0) < seq
    dq, dk, dv = [], [], []
    for h in range(heads):
        q, k, v, dm = qkv[h], qkv[heads + h], qkv[2 * heads + h], dmix[h]
        p = jnp.where(mask, jnp.exp2(dot_tn(k, q) * c - lse[h : h + 1, :]), 0.0)
        dp = dot_tn(v, dm)
        delta = jnp.sum(p * dp, axis=0, keepdims=True)
        ds = (p * (dp - delta)).astype(LOW)
        dq.append(dot_nn(k, ds) * scale)
        dk.append(dot_nt(q, ds) * scale)
        dv.append(dot_nt(dm, p.astype(LOW)))
    for j, part in enumerate((dq, dk, dv)):
        dqkv[j * share : (j + 1) * share, :] = jnp.concatenate(part, axis=0).astype(LOW)
    gain1, shift1 = vec[:, 0:1], vec[:, 1:2]
    for at in lanes(count):
        part = dot_nn(w[...], dqkv[:, at])
        keep_o[:, at] = part[:share]
        keep_y[:, at] = part[share : 2 * share]
        send[0, :, at] = part[2 * share : 3 * share].astype(LOW)
        send[1, :, at] = part[3 * share :].astype(LOW)
        stats[0:1, at] = jnp.sum(part * gain1, axis=0, keepdims=True)
        stats[1:2, at] = jnp.sum(part * (attn_in[:, at].astype(F32) - shift1), axis=0, keepdims=True)
    sums_qkv[...] = dot_nt(jnp.ones((8, count), LOW), dqkv[...])


def out_kernel(live, base, came, across, out):
    seq = out.shape[2]
    rows = base[0] + came[0, 0].astype(F32) + across[0].astype(F32)
    out[0] = (rows * live[pl.program_id(0)])[:, :seq].astype(LOW)


def grad_kernel(h_grad, keep, came, across, x_own, stats1, stats, vec, _, out, sums):
    share, seq = out.shape
    ng = keep[...] + came[0].astype(F32) + across[...].astype(F32)
    inverse = stats1[1:2, :]
    n1 = (x_own[...].astype(F32) - stats1[0:1, :]) * inverse
    mean = stats[...] * (1.0 / (4 * share))
    rows = h_grad[...] + inverse * (ng * vec[:, 0:1] - mean[0:1] - n1 * mean[1:2])
    out[...] = rows[:, :seq].astype(LOW)
    sums[...] = column(
        [jnp.sum(ng * n1, axis=1, keepdims=True), jnp.sum(ng, axis=1, keepdims=True)]
    )


def weight_grad_kernel(count, *refs):
    a, b, out = refs[1 : count + 1], refs[count + 1 : 2 * count + 1], refs[-1]
    total = dot_nt(a[0][...], b[0][...])
    for i in range(1, count):
        total = total + dot_nt(a[i][...], b[i][...])
    out[0] = total.astype(LOW)


def weight_split_kernel(count, *refs):
    odd, a, b = refs[1][0] == 1, refs[2 : count + 2], refs[count + 2 : 2 * count + 2]
    keep, send = refs[-2:]
    total = dot_nt(a[0][...], b[0][...])
    for i in range(1, count):
        total = total + dot_nt(a[i][...], b[i][...])
    half = total.shape[0] // 2
    top, low = total[:half], total[half:]
    keep[0] = jnp.where(odd, low, top)
    send[0] = jnp.where(odd, top, low).astype(LOW)


def shaped(*dims, dtype=LOW):
    return jax.ShapeDtypeStruct(dims, dtype)


def spec_of(array):
    if isinstance(array, tuple):
        array, i = array
        zeros = (0,) * (len(array.shape) - 1)
        return pl.BlockSpec(
            (None, *array.shape[1:]), lambda _: (i, *zeros), pipeline_mode=pl.Buffered(1)
        )
    zeros = (0,) * len(array.shape)
    return pl.BlockSpec(array.shape, lambda _: zeros, pipeline_mode=pl.Buffered(1))


SCALARS = pl.BlockSpec(memory_space=pltpu.SMEM)
LEFT = pl.BlockSpec(memory_space=pl.ANY)


def array_of(array):
    return array[0] if isinstance(array, tuple) else array


def run(kernel, outs, args, name, flops, scratch=(), after=(), scalars=0, buffers=None):
    arrays = [array_of(a) for a in args]
    shapes = [array_of(o) for o in outs]
    moved = sum(math.prod(a.shape) * a.dtype.itemsize for a in [*arrays, *shapes])
    buffers = buffers or {}
    used, extra = len(args), len(buffers) + len(after)

    def body(*refs):
        kernel(*refs[:used], *refs[used + extra :])

    return pl.pallas_call(
        body,
        grid=(1,),
        out_shape=tuple(shapes),
        in_specs=[*[SCALARS] * scalars, *map(spec_of, args[scalars:]), *[LEFT] * extra],
        out_specs=tuple(map(spec_of, outs)),
        input_output_aliases={used + j: o for j, o in enumerate(buffers)},
        scratch_shapes=scratch,
        compiler_params=pltpu.CompilerParams(vmem_limit_bytes=VMEM_LIMIT),
        cost_estimate=pl.CostEstimate(flops=flops, bytes_accessed=moved, transcendentals=0),
        name=name,
    )(*arrays, *buffers.values(), *after)


def prepare(array, bias, count):
    slots, share, _ = array.shape
    return run(prepare_kernel, [shaped(slots, share, count)], [array, bias], "prepare", 10**6)[0]


def prepare_grad(array, live, count, after=()):
    slots, share, _ = array.shape
    outs = [shaped(slots, share, count), shaped(8, share, dtype=F32)]
    return run(
        prepare_grad_kernel, outs, [live, array], "prepare", 10**6, after=after, scalars=1
    )


def attn_fwd(x, i, vec, w, bias, seq, after=()):
    slots, share, count = x[0].shape
    outs = [
        shaped(4 * share, count),
        shaped(3 * share // HDIM, HDIM, count),
        shaped(share, count),
        shaped(8, count, dtype=F32),
        shaped(8, count, dtype=F32),
    ]
    flops = 2 * count * 12 * share * share + 8 * count * count * 256
    return run(
        functools.partial(attn_fwd_kernel, seq), outs, [*[(a, i) for a in x], vec, w, bias],
        "attn_fwd", flops, after=after,
    )


def mlp_fwd(x, m, i, vec, w_out, up, up_bias, down, seq, buffers, after=()):
    slots, share, count = x[0].shape
    hidden = up.shape[0]
    outs = [
        shaped(4 * share, count),
        shaped(4 * share, count),
        shaped(hidden, count),
        shaped(hidden, count),
        (shaped(slots, share, count, dtype=F32), i),
        shaped(8, count, dtype=F32),
        (shaped(slots, share, count, dtype=F32), i),
        (shaped(slots, 2, share, count), i),
    ]
    flops = 2 * count * 4 * share * (4 * share + 2 * hidden)
    args = [*[(a, i) for a in x], *m, vec, w_out, up, up_bias, down]
    return run(
        functools.partial(mlp_fwd_kernel, seq), outs, args, "mlp_fwd", flops,
        after=after, buffers=buffers,
    )


def mlp_bwd(c, i, slope, down, up, after=()):
    _, share, count = c[0].shape
    hidden = up.shape[1]
    outs = [
        shaped(4 * share, count),
        shaped(hidden, count),
        shaped(2, share, count, dtype=F32),
        shaped(2, share, count),
        shaped(8, hidden, dtype=F32),
    ]
    flops = 2 * count * 4 * share * 2 * hidden
    args = [*[(a, i) for a in c], slope, down, up]
    return run(mlp_bwd_kernel, outs, args, "mlp_bwd", flops, after=after)


def attn_bwd(ng, cot, norm2, stats2, vec, w_out, qkv, lse, w, attn_in, seq, after=()):
    width, count = cot.shape
    share = width // 4
    outs = [
        shaped(width, count),
        shaped(share, count, dtype=F32),
        shaped(3 * share, count),
        shaped(share, count, dtype=F32),
        shaped(share, count, dtype=F32),
        shaped(2, share, count),
        shaped(8, count, dtype=F32),
        shaped(share, 8, dtype=F32),
        shaped(8, 3 * share, dtype=F32),
    ]
    flops = 2 * count * 16 * share * share + 20 * count * count * 256
    args = [*ng, cot, norm2, stats2, vec, w_out, qkv, lse, w, attn_in]
    scratch = (pltpu.VMEM((share // HDIM, HDIM, count), LOW),)
    return run(
        functools.partial(attn_bwd_kernel, seq), outs, args, "attn_bwd", flops, scratch, after
    )


def finish_grad(args, i, buffer, slots, seq):
    share = args[0].shape[0]
    outs = [(shaped(slots, share, seq), i), shaped(share, 8, dtype=F32)]
    buffers = {} if buffer is None else {0: buffer}

    def kernel(*refs):
        grad_kernel(*refs[:8], None, *refs[8:])

    return run(kernel, outs, args, "grad", 10**6, buffers=buffers)


def finish_out(live, base, came, across, seq):
    slots, share, count = base.shape
    return pl.pallas_call(
        out_kernel,
        grid=(slots,),
        out_shape=shaped(slots, share, seq),
        in_specs=[
            SCALARS,
            pl.BlockSpec((1, share, count), lambda i: (i, 0, 0)),
            pl.BlockSpec((1, 1, share, count), lambda i: (i, 0, 0, 0)),
            pl.BlockSpec((1, share, count), lambda i: (i, 0, 0)),
        ],
        out_specs=pl.BlockSpec((1, share, seq), lambda i: (i, 0, 0)),
        compiler_params=pltpu.CompilerParams(vmem_limit_bytes=VMEM_LIMIT),
        name="out",
    )(live, base, came, across)


def place(near, far, pos):
    count = 2 * len(near)
    rows, hidden = near[0].shape
    outs = [shaped(count, rows, hidden), shaped(hidden, count * rows)]
    placed, turned = run(place_kernel, outs, [pos, *near, far], "place", 10**6, scalars=1)
    return placed.reshape(count * rows, hidden), turned


def join(near, far):
    rows, half = near.shape
    outs = [shaped(rows, 2 * half), shaped(half // 2, rows)]
    return run(join_kernel, outs, [near, far], "join", 10**6)


def weight_grad(a, b, order, after=()):
    width, count = a[0].shape
    share, hidden = width // 4, b[0].shape[0]
    slots = len(a)
    out = shaped(4, share, hidden)
    moved = sum(math.prod(v.shape) * 2 for v in [*a, *b, out])
    out = pl.pallas_call(
        lambda *refs: weight_grad_kernel(slots, *refs),
        out_shape=out,
        grid_spec=pltpu.PrefetchScalarGridSpec(
            num_scalar_prefetch=1,
            grid=(4,),
            in_specs=[
                *[pl.BlockSpec((share, count), lambda r, order: (r, 0)) for _ in a],
                *[pl.BlockSpec((hidden, count), lambda r, order: (0, 0)) for _ in b],
                *[pl.BlockSpec(memory_space=pl.ANY)] * len(after),
            ],
            out_specs=pl.BlockSpec((1, share, hidden), lambda r, order: (order[r], 0, 0)),
        ),
        compiler_params=pltpu.CompilerParams(vmem_limit_bytes=VMEM_LIMIT),
        cost_estimate=pl.CostEstimate(
            flops=2 * slots * width * hidden * count, bytes_accessed=moved, transcendentals=0
        ),
        name="weight_grad",
    )(order, *a, *b, *after)
    return out.reshape(width, hidden)


def weight_split(a, b, order, odd, after=()):
    width, count = a[0].shape
    share, hidden = width // 4, b[0].shape[0]
    slots = len(a)
    outs = [shaped(4, share // 2, hidden, dtype=F32), shaped(4, share // 2, hidden)]
    moved = sum(math.prod(v.shape) * 2 for v in [*a, *b, *outs])
    return pl.pallas_call(
        lambda *refs: weight_split_kernel(slots, *refs),
        out_shape=outs,
        grid_spec=pltpu.PrefetchScalarGridSpec(
            num_scalar_prefetch=2,
            grid=(4,),
            in_specs=[
                *[pl.BlockSpec((share, count), lambda r, order, odd: (r, 0)) for _ in a],
                *[pl.BlockSpec((hidden, count), lambda r, order, odd: (0, 0)) for _ in b],
                *[pl.BlockSpec(memory_space=pl.ANY)] * len(after),
            ],
            out_specs=[
                pl.BlockSpec((1, share // 2, hidden), lambda r, order, odd: (order[r], 0, 0))
            ]
            * 2,
        ),
        compiler_params=pltpu.CompilerParams(vmem_limit_bytes=VMEM_LIMIT),
        cost_estimate=pl.CostEstimate(
            flops=2 * slots * width * hidden * count, bytes_accessed=moved, transcendentals=0
        ),
        name="weight_grad",
    )(order, odd, *a, *b, *after)


def place_blocks_kernel(order, value, out, turned):
    for r in range(4):
        out[r] = value[order[r]]
    rows = out.shape[0] * out.shape[1]
    turned[...] = out[...].reshape(rows, out.shape[2]).T


def place_blocks(value, t):
    rows, hidden = value.shape
    order = jnp.stack([t ^ m for m in (0, 2, 1, 3)]).astype(jnp.int32)
    placed, turned = run(
        place_blocks_kernel,
        [shaped(4, rows // 4, hidden), shaped(hidden, rows)],
        [order, value.reshape(4, rows // 4, hidden)],
        "place",
        10**6,
        scalars=1,
    )
    return placed.reshape(rows, hidden), turned


def gate(values, after):
    values, _ = lax.optimization_barrier((list(values), list(after)))
    return values


def dp_swap(value, mask):
    size = lax.axis_size("dp")
    return lax.ppermute(value, "dp", [(i, i ^ mask) for i in range(size)])


def gather_dp_whole(shard, t):
    size = lax.axis_size("dp")
    value = lax.all_gather(shard, "dp", axis=0, tiled=True)
    if size != 8:
        value = rel_blocks(value, t)
        return value, value.T
    return place_blocks(value, t)


def gather_first(shard):
    return [shard, *[dp_swap(shard, m) for m in (2, 4, 6)]]


def gather_second(near, far, t):
    pos = []
    for m in range(8):
        k = lax.axis_index("dp") ^ m
        b = t ^ (k >> 1)
        pos.append((((b & 1) << 1) | (b >> 1)) * 2 + (k & 1))
    return place(near, far, jnp.stack(pos).astype(jnp.int32))


def scatter_dp(a, b, t, direct, after=()):
    size = lax.axis_size("dp")
    order = jnp.stack([t ^ m for m in (0, 2, 1, 3)]).astype(jnp.int32)
    if size != 8 or not direct:
        value = weight_grad(a, b, order, after)
        return lax.psum_scatter(value, "dp", scatter_dimension=0, tiled=True).astype(F32)
    me = lax.axis_index("dp")
    keep, send = weight_split(a, b, order ^ (me >> 1), (me & 1).reshape(1).astype(jnp.int32), after)
    total = keep + dp_swap(send, 1).astype(F32)
    out = total[0]
    for j in (1, 2, 3):
        out = out + dp_swap(total[j].astype(LOW), 2 * j).astype(F32)
    return out


def sum_dp(value):
    size = lax.axis_size("dp")
    if size != 8:
        return lax.psum(value, "dp")
    value = value + dp_swap(value, 1)
    return sum((dp_swap(value, m) for m in (2, 4, 6)), value)


def columns(vectors, count=8):
    vectors = [*vectors, *[jnp.zeros_like(vectors[0])] * (count - len(vectors))]
    return jnp.stack(vectors, axis=1)


def local(
    images,
    image_count,
    attn_gain,
    attn_shift,
    query_weight,
    query_bias,
    key_weight,
    value_weight,
    value_bias,
    output_weight,
    output_bias,
    mlp_gain,
    mlp_shift,
    up_weight,
    up_bias,
    down_weight,
    down_bias,
    cotangent,
):
    images, cotangent = images.transpose(0, 2, 1), cotangent.transpose(0, 2, 1)
    slots, share, seq = images.shape
    t = lax.axis_index("tensor")
    count = -(-seq // TILE) * TILE
    zero = jnp.zeros_like(output_bias)
    gains = [rel_blocks(a, t) for a in (attn_gain, attn_shift, mlp_gain, mlp_shift)]
    down_rows = jnp.concatenate([down_bias, zero, zero, zero])
    vec = columns([gains[0], gains[1], gains[1], gains[2], gains[3], down_rows])
    vec_own = vec[:share]
    qkv_bias = columns([jnp.concatenate([query_bias, zero, value_bias])])
    up_b = columns([up_bias])
    live = (jnp.arange(slots) < image_count[0]).astype(F32)

    fast = lax.axis_size("dp") == 8
    qkv_shard = jnp.concatenate([query_weight, key_weight, value_weight], axis=1)
    out_t = output_weight.T
    out_shard = jnp.concatenate([out_t, y_swap(out_t)], axis=1)
    x_own = prepare(images, columns([output_bias]), count)
    x_across = y_swap(*gate([x_own], [out_shard]))
    up_value = lax.all_gather(up_weight, "dp", axis=0, tiled=True)
    cot_own, cot_sums = prepare_grad(cotangent, live, count, [x_own])
    if fast:
        near = gather_first(*gate([qkv_shard], [x_own]))
        near_stack, out_shard = gate([jnp.stack(near), out_shard], near[1:])
        far = dp_swap(near_stack, 1)
        out_near = gather_first(out_shard)
        x_across, x_own2, cot_send = gate([x_across, x_own, cot_own], near[1:])
        (down_shard, cot_send) = gate([down_weight.T, cot_send], [*out_near[1:], x_across])
        down_near = gather_first(down_shard)
        qkv_w, qkv_t = gather_second(near, far, t)
    else:
        x_own2, cot_send = x_own, cot_own
        qkv_w, qkv_t = gather_dp_whole(qkv_shard, t)
    cot_across = y_swap(cot_send)
    x = [x_own, x_across, core_swap(x_own2), core_swap(x_across)]
    fwd, mixes = [], []
    for i in range(slots):
        after = [fwd[i - 1][4]] if i else [cot_sums]
        if i == 0 and fast:
            (out_stack,) = gate([jnp.stack(out_near)], [far])
            out_far = dp_swap(out_stack, 1)
        if i == 2 and fast:
            out_far, down_stack = gate([out_far, jnp.stack(down_near)], after)
            down_far = dp_swap(down_stack, 1)
        fwd.append(attn_fwd(x, i, vec, qkv_t, qkv_bias, seq, after))
        mixes.append([fwd[i][2], y_swap(fwd[i][2])])
    if fast:
        (o_half, _) = gather_second(out_near, out_far, t)
        down_t, down_w = gather_second(down_near, down_far, t)
        up_w, up_t = place_blocks(up_value, t)
    else:
        o_half, _ = gather_dp_whole(out_shard, t)
        down_t, down_w = gather_dp_whole(down_weight.T, t)
        up_w, up_t = gather_dp_whole(up_weight, t)
    o_full, o_mine = join(o_half, core_swap(o_half))
    for m in mixes:
        m.extend([core_swap(m[0]), core_swap(m[1])])
    (cot_across,) = gate([cot_across], [fwd[-1][2]])
    cot = [cot_own, cot_across, core_swap(cot_own), core_swap(cot_across)]

    mlp, back, ends = [], [], []
    norm2_grad = []
    last = [fwd[-1][4]]

    def attention_back(i, after):
        attn_in, qkv, _, stats1, lse = fwd[i]
        norm2, stats2 = mlp[i][1], mlp[i][5]
        ends.append(
            attn_bwd(
                norm2_grad[i], back[i][0], norm2, stats2, vec, o_mine, qkv, lse, qkv_w, attn_in,
                seq, after,
            )
        )

    for i in range(slots):
        buffers = {j: mlp[i - 1][j] for j in (4, 6, 7)} if i else {}
        mlp.append(mlp_fwd(x, mixes[i], i, vec, o_full, up_t, up_b, down_t, seq, buffers, last))
        if i:
            half, across = norm2_grad[i - 1]
            both = (half + across.astype(F32)).astype(LOW)
            (both,) = gate([both], [mlp[i][5]])
            norm2_grad[i - 1] = (half, across, core_swap(both))
        back.append(mlp_bwd(cot, i, mlp[i][3], down_w, up_w, [mlp[i][5]]))
        half = back[i][2] + core_swap(back[i][3]).astype(F32)
        norm2_grad.append((half, y_swap(half[::-1].astype(LOW))))
        last = [half]
    down_grad = scatter_dp([b[0] for b in back], [m[2] for m in mlp], t, True, last).T
    base, keep, send = (mlp[-1][j] for j in (4, 6, 7))
    came = core_swap(*gate([send], last))
    across = y_swap((keep + came[:, 1].astype(F32)).astype(LOW))
    out_buffer = finish_out(live, base, came, across, seq)
    up_grad = scatter_dp([m[0] for m in mlp], [b[1] for b in back], t, False, last)
    for i in range(slots):
        attention_back(i, last)
        last = [ends[i][-1]]
        if i == 0:
            half, across = norm2_grad[-1]
            both = (half + across.astype(F32)).astype(LOW)
            (both,) = gate([both], last)
            norm2_grad[-1] = (half, across, core_swap(both))
    mixed_rows = [f[2] for f in fwd]
    qkv_grad = scatter_dp([f[0] for f in fwd], [e[2] for e in ends], t, True)
    out_grad = scatter_dp([e[0] for e in ends], mixed_rows, t, True).T
    grad_buffer, sums = None, None
    for group in (list(range(slots - 1)), [slots - 1]):
        came = [core_swap(ends[i][5]) for i in group]
        across = y_swap(
            jnp.stack([(ends[i][4] + c[1].astype(F32)).astype(LOW) for i, c in zip(group, came)])
        )
        stats = jnp.stack([ends[i][6] for i in group])
        stats = stats + core_swap(stats)
        stats = stats + y_swap(stats)
        for j, i in enumerate(group):
            grad_buffer, grad_sums = finish_grad(
                [ends[i][1], ends[i][3], came[j], (across, j), (x_own, i), fwd[i][3], (stats, j), vec_own],
                i, grad_buffer, slots, seq,
            )
            now = (grad_sums, ends[i][7], ends[i][8], back[i][-1])
            sums = now if sums is None else jax.tree.map(jnp.add, sums, now)
    sums = (*sums, cot_sums)
    sizes = [2 * share, 3 * share, 3 * share, up_bias.shape[0], share]
    small = jnp.concatenate(
        [
            sums[0][:, :2].T.reshape(-1),
            sums[1][:, :3].T.reshape(-1),
            sums[2][0],
            sums[3][0],
            sums[4][0],
        ]
    )
    small = sum_dp(small)
    parts, at = [], 0
    for size in sizes:
        parts.append(small[at : at + size])
        at += size
    grad_sums, own_sums = parts[0].reshape(2, share), parts[1].reshape(3, share)
    qkv_sums, up_sum, cot_sum = parts[2:]
    return (
        out_buffer.transpose(0, 2, 1),
        grad_buffer.transpose(0, 2, 1),
        grad_sums[0],
        grad_sums[1],
        qkv_grad[:, :share],
        qkv_sums[:share],
        qkv_grad[:, share : 2 * share],
        qkv_grad[:, 2 * share :],
        qkv_sums[2 * share :],
        out_grad,
        own_sums[0],
        own_sums[1],
        own_sums[2],
        up_grad,
        up_sum,
        down_grad,
        cot_sum,
    )


def solution(mesh):
    in_specs = (
        P("dp", None, "tensor"),
        P("dp"),
        P(),
        P(),
        P("dp", "tensor"),
        P("tensor"),
        P("dp", "tensor"),
        P("dp", "tensor"),
        P("tensor"),
        P("tensor", "dp"),
        P("tensor"),
        P(),
        P(),
        P("dp", "tensor"),
        P("tensor"),
        P("tensor", "dp"),
        P("tensor"),
        P("dp", None, "tensor"),
    )
    out_specs = (
        P("dp", None, "tensor"),
        P("dp", None, "tensor"),
        P("tensor"),
        P("tensor"),
        P("dp", "tensor"),
        P("tensor"),
        P("dp", "tensor"),
        P("dp", "tensor"),
        P("tensor"),
        P("tensor", "dp"),
        P("tensor"),
        P("tensor"),
        P("tensor"),
        P("dp", "tensor"),
        P("tensor"),
        P("tensor", "dp"),
        P("tensor"),
    )
    return jax.shard_map(local, mesh=mesh, in_specs=in_specs, out_specs=out_specs, check_vma=False)
```

```python
import functools
import math

import jax
import jax.numpy as jnp
from jax import lax
from jax.experimental import pallas as pl
from jax.experimental.pallas import tpu as pltpu
from jax.sharding import PartitionSpec as P

HDIM = 72
EPSILON = 1e-06
LOG2E = 1.4426950408889634
MASKED = -1e30
GELU_A = math.sqrt(2.0 / math.pi)
GELU_B = 0.044715
TILE = 256
VMEM_LIMIT = 56 * 2**20
F32 = jnp.float32
LOW = jnp.bfloat16
Y_SWAP = [(0, 2), (2, 0), (1, 3), (3, 1)]
CORE_SWAP = [(0, 1), (1, 0), (2, 3), (3, 2)]


def y_swap(value):
    return lax.ppermute(value, "tensor", Y_SWAP)


def core_swap(value):
    return lax.ppermute(value, "tensor", CORE_SWAP)


def dot_nn(a, b):
    return lax.dot_general(a, b, (((1,), (0,)), ((), ())), preferred_element_type=F32)


def dot_nt(a, b):
    return lax.dot_general(a, b, (((1,), (1,)), ((), ())), preferred_element_type=F32)


def dot_tn(a, b):
    return lax.dot_general(a, b, (((0,), (0,)), ((), ())), preferred_element_type=F32)


def rel_blocks(value, t):
    width = value.shape[0] // 4
    return jnp.concatenate(
        [lax.dynamic_slice_in_dim(value, (t ^ m) * width, width, 0) for m in (0, 2, 1, 3)], axis=0
    )


def rows4(a, b, c, d):
    return jnp.concatenate([a, b, c, d], axis=0)


def lanes(count):
    return [slice(at, at + TILE) for at in range(0, count, TILE)]


def column(sums):
    pad = jnp.zeros((sums[0].shape[0], 8 - len(sums)), F32)
    return jnp.concatenate([*sums, pad], axis=1)


def prepare_kernel(x, bias, out):
    slots, share, seq = x.shape
    high = bias[:, 0:1].astype(LOW)
    rest = bias[:, 0:1] - high.astype(F32)
    mid = rest.astype(LOW)
    for i in range(slots):
        out[i] = jnp.zeros(out.shape[1:], LOW)
        out[i, :, :seq] = x[i]
        out[i, :, seq : seq + 1] = high
        out[i, :, seq + 1 : seq + 2] = mid
        out[i, :, seq + 2 : seq + 3] = (rest - mid.astype(F32)).astype(LOW)


def prepare_grad_kernel(live, x, out, sums):
    slots, share, seq = x.shape
    total = 0.0
    for i in range(slots):
        out[i] = jnp.zeros(out.shape[1:], LOW)
        out[i, :, :seq] = (x[i].astype(F32) * live[i]).astype(LOW)
        total = total + dot_nt(jnp.ones((8, out.shape[2]), LOW), out[i])
    sums[...] = total


def place_pair_kernel(pos, *refs):
    count = len(refs) - 4
    far, first, second, turned = refs[count:]
    cut = first.shape[2]
    for m in range(count):
        first[pos[2 * m]] = refs[m][:, :cut]
        first[pos[2 * m + 1]] = far[m, :, :cut]
        second[pos[2 * m]] = refs[m][:, cut:]
        second[pos[2 * m + 1]] = far[m, :, cut:]
    rows = second.shape[0] * second.shape[1]
    turned[...] = second[...].reshape(rows, second.shape[2]).T


def place_kernel(pos, *refs):
    count = len(refs) - 3
    far, out, turned = refs[count:]
    for m in range(count):
        out[pos[2 * m]] = refs[m][...]
        out[pos[2 * m + 1]] = far[m]
    rows = out.shape[0] * out.shape[1]
    turned[...] = out[...].reshape(rows, out.shape[2]).T


def join_kernel(near, far, out, turned):
    rows, half = near.shape
    out[:, :half] = near[...]
    out[: rows // 2, half:] = far[rows // 2 :]
    out[rows // 2 :, half:] = far[: rows // 2]
    turned[...] = near[:, : half // 2].T


def attn_fwd_kernel(seq, xo, xy, xc, xd, vec, w, bias, attn_in, qkv, mixed, stats, lse):
    share, count = xo.shape
    heads = share // HDIM
    gain, shift = vec[:, 0:1], vec[:, 1:2]
    for at in lanes(count):
        x = rows4(xo[:, at], xy[:, at], xc[:, at], xd[:, at]).astype(F32)
        mean = jnp.mean(x, axis=0, keepdims=True)
        centred = x - mean
        inverse = lax.rsqrt(jnp.mean(centred * centred, axis=0, keepdims=True) + EPSILON)
        low = (centred * inverse * gain + shift).astype(LOW)
        attn_in[:, at] = low
        stats[0:1, at] = mean
        stats[1:2, at] = inverse
        part = dot_nn(w[...], low) + bias[:, 0:1]
        for i in range(3 * heads):
            qkv[i, :, at] = part[i * HDIM : (i + 1) * HDIM].astype(LOW)
    c = LOG2E / math.sqrt(HDIM)
    mask = lax.broadcasted_iota(jnp.int32, (count, 1), 0) < seq
    out = []
    for h in range(heads):
        q, k, v = qkv[h], qkv[heads + h], qkv[2 * heads + h]
        s = jnp.where(mask, dot_tn(k, q), MASKED)
        top = jnp.max(s, axis=0, keepdims=True)
        e = jnp.exp2((s - top) * c)
        total = jnp.sum(e, axis=0, keepdims=True)
        lse[h : h + 1, :] = top * c + jnp.log2(total)
        out.append(dot_nn(v, e.astype(LOW)) * (1.0 / total))
    mixed[...] = jnp.concatenate(out, axis=0).astype(LOW)


def mlp_fwd_kernel(
    seq, xo, xy, xc, xd, mo, my, mc, md, vec, w_out, up, up_bias, down,
    mlp_in, norm2, activ, slope, base, stats, keep, send,
):
    share, count = xo.shape
    gain, shift = vec[:, 3:4], vec[:, 4:5]
    tail = rows4(xo[:, seq:], xy[:, seq:], xc[:, seq:], xd[:, seq:]).astype(F32)
    o_bias = tail[:, 0:1] + tail[:, 1:2] + tail[:, 2:3]
    for at in lanes(count):
        mixed = rows4(mo[:, at], my[:, at], mc[:, at], md[:, at])
        x = rows4(xo[:, at], xy[:, at], xc[:, at], xd[:, at]).astype(F32)
        hidden = x + dot_nn(w_out[...], mixed) + o_bias
        mean = jnp.mean(hidden, axis=0, keepdims=True)
        centred = hidden - mean
        inverse = lax.rsqrt(jnp.mean(centred * centred, axis=0, keepdims=True) + EPSILON)
        normed = centred * inverse
        stats[0:1, at] = inverse
        norm2[:, at] = normed.astype(LOW)
        low = (normed * gain + shift).astype(LOW)
        mlp_in[:, at] = low
        v = dot_nn(up[...], low) + up_bias[:, 0:1]
        square = v * v
        tanh = jnp.tanh(v * (GELU_A + GELU_A * GELU_B * square))
        gate = 0.5 + 0.5 * tanh
        act = (v * gate).astype(LOW)
        activ[:, at] = act
        slope[:, at] = (
            gate + v * (0.5 - 0.5 * tanh * tanh) * (GELU_A + 3.0 * GELU_A * GELU_B * square)
        ).astype(LOW)
        part = dot_nn(down[...], act)
        base[:, at] = hidden[:share] + part[:share] + vec[:share, 5:6]
        keep[:, at] = part[share : 2 * share]
        send[0, :, at] = part[2 * share : 3 * share].astype(LOW)
        send[1, :, at] = part[3 * share :].astype(LOW)


def mlp_bwd_kernel(co, cy, cc, cd, slope, down, up, cot, pre_grad, keep, send, sums):
    share, count = co.shape
    for at in lanes(count):
        c = rows4(co[:, at], cy[:, at], cc[:, at], cd[:, at])
        cot[:, at] = c
        low = (dot_nn(down[...], c) * slope[:, at].astype(F32)).astype(LOW)
        pre_grad[:, at] = low
        part = dot_nn(up[...], low)
        keep[0, :, at] = part[:share]
        keep[1, :, at] = part[share : 2 * share]
        send[0, :, at] = part[2 * share : 3 * share].astype(LOW)
        send[1, :, at] = part[3 * share :].astype(LOW)
    sums[...] = dot_nt(jnp.ones((8, count), LOW), pre_grad[...])


def attn_bwd_kernel(
    seq, half, across, far, cot, norm2, stats2, vec, w_out, qkv, lse, w, attn_in,
    branch, h_grad, dqkv, keep_o, keep_y, send, stats, sums_own, sums_qkv,
    dmix,
):
    width, count = cot.shape
    share = width // 4
    heads = share // HDIM
    gain2 = vec[:, 3:4]
    sums = [0.0, 0.0, 0.0]
    for at in lanes(count):
        near = half[:, :, at] + across[:, :, at].astype(F32)
        ng = rows4(near[0], near[1], far[0, :, at].astype(F32), far[1, :, at].astype(F32))
        n2 = norm2[:, at].astype(F32)
        g = ng * gain2
        first = jnp.mean(g, axis=0, keepdims=True)
        second = jnp.mean(g * n2, axis=0, keepdims=True)
        hg = cot[:, at].astype(F32) + stats2[0:1, at] * (g - first - n2 * second)
        h_grad[:, at] = hg[:share]
        low = hg.astype(LOW)
        branch[:, at] = low
        dm = dot_nn(w_out[...], low)
        for h in range(heads):
            dmix[h, :, at] = dm[h * HDIM : (h + 1) * HDIM].astype(LOW)
        own = ng[:share]
        now = [hg[:share], own * n2[:share], own]
        sums = [a + jnp.sum(b, axis=1, keepdims=True) for a, b in zip(sums, now)]
    sums_own[...] = column(sums)
    scale = 1.0 / math.sqrt(HDIM)
    c = LOG2E * scale
    mask = lax.broadcasted_iota(jnp.int32, (count, 1), 0) < seq
    dq, dk, dv = [], [], []
    for h in range(heads):
        q, k, v, dm = qkv[h], qkv[heads + h], qkv[2 * heads + h], dmix[h]
        p = jnp.where(mask, jnp.exp2(dot_tn(k, q) * c - lse[h : h + 1, :]), 0.0)
        dp = dot_tn(v, dm)
        delta = jnp.sum(p * dp, axis=0, keepdims=True)
        ds = (p * (dp - delta)).astype(LOW)
        dq.append(dot_nn(k, ds) * scale)
        dk.append(dot_nt(q, ds) * scale)
        dv.append(dot_nt(dm, p.astype(LOW)))
    for j, part in enumerate((dq, dk, dv)):
        dqkv[j * share : (j + 1) * share, :] = jnp.concatenate(part, axis=0).astype(LOW)
    gain1, shift1 = vec[:, 0:1], vec[:, 1:2]
    for at in lanes(count):
        part = dot_nn(w[...], dqkv[:, at])
        keep_o[:, at] = part[:share]
        keep_y[:, at] = part[share : 2 * share]
        send[0, :, at] = part[2 * share : 3 * share].astype(LOW)
        send[1, :, at] = part[3 * share :].astype(LOW)
        stats[0:1, at] = jnp.sum(part * gain1, axis=0, keepdims=True)
        stats[1:2, at] = jnp.sum(part * (attn_in[:, at].astype(F32) - shift1), axis=0, keepdims=True)
    sums_qkv[...] = dot_nt(jnp.ones((8, count), LOW), dqkv[...])


def out_kernel(live, base, came, across, out):
    seq = out.shape[2]
    rows = base[0] + came[0, 0].astype(F32) + across[0].astype(F32)
    out[0] = (rows * live[pl.program_id(0)])[:, :seq].astype(LOW)


def grad_kernel(h_grad, keep, came, across, x_own, stats1, stats, vec, _, out, sums):
    share, seq = out.shape
    ng = keep[...] + came[0].astype(F32) + across[...].astype(F32)
    inverse = stats1[1:2, :]
    n1 = (x_own[...].astype(F32) - stats1[0:1, :]) * inverse
    mean = stats[...] * (1.0 / (4 * share))
    rows = h_grad[...] + inverse * (ng * vec[:, 0:1] - mean[0:1] - n1 * mean[1:2])
    out[...] = rows[:, :seq].astype(LOW)
    sums[...] = column(
        [jnp.sum(ng * n1, axis=1, keepdims=True), jnp.sum(ng, axis=1, keepdims=True)]
    )


def weight_grad_kernel(count, *refs):
    a, b, out = refs[1 : count + 1], refs[count + 1 : 2 * count + 1], refs[-1]
    total = dot_nt(a[0][...], b[0][...])
    for i in range(1, count):
        total = total + dot_nt(a[i][...], b[i][...])
    out[0] = total.astype(LOW)


def row_sum(pairs, start):
    total = None if start is None else start[...]
    for a, b in pairs:
        part = dot_nt(a[...], b[...])
        total = part if total is None else total + part
    return total


def weight_part_kernel(count, *refs):
    refs[-1][...] = row_sum(list(zip(refs[:count], refs[count : 2 * count])), None)


def weight_split_kernel(counts, starts, *refs):
    odd, refs = refs[1][0] == 1, list(refs[2:])
    keep, send = refs[-2:]
    at = 0
    for count, start in zip(counts, starts):
        pairs = list(zip(refs[:count], refs[count : 2 * count]))
        total = row_sum(pairs, refs[2 * count] if start else None)
        refs = refs[2 * count + start :]
        half = total.shape[0] // 2
        top, low = total[:half], total[half:]
        to = at + total.shape[1]
        keep[0, :, at:to] = jnp.where(odd, low, top)
        send[0, :, at:to] = jnp.where(odd, top, low).astype(LOW)
        at = to


TIMES = {
    "prepare": 2.6,
    "place": 4.0,
    "join": 4.0,
    "attn_fwd": 10.0,
    "mlp_fwd": 19.5,
    "mlp_bwd": 11.0,
    "attn_bwd": 17.7,
    "weight_grad": 12.4,
    "weight_part": 7.0,
    "grad": 3.3,
}
RATE = 2e8


def cost(name):
    return pl.CostEstimate(
        flops=int(TIMES[name] * RATE), bytes_accessed=0, transcendentals=0
    )


def shaped(*dims, dtype=LOW):
    return jax.ShapeDtypeStruct(dims, dtype)


def spec_of(array):
    if isinstance(array, tuple):
        array, i = array
        zeros = (0,) * (len(array.shape) - 1)
        return pl.BlockSpec(
            (None, *array.shape[1:]), lambda _: (i, *zeros), pipeline_mode=pl.Buffered(1)
        )
    zeros = (0,) * len(array.shape)
    return pl.BlockSpec(array.shape, lambda _: zeros, pipeline_mode=pl.Buffered(1))


SCALARS = pl.BlockSpec(memory_space=pltpu.SMEM)
LEFT = pl.BlockSpec(memory_space=pl.ANY)


def array_of(array):
    return array[0] if isinstance(array, tuple) else array


def run(kernel, outs, args, name, flops, scratch=(), after=(), scalars=0, buffers=None):
    arrays = [array_of(a) for a in args]
    shapes = [array_of(o) for o in outs]
    moved = sum(math.prod(a.shape) * a.dtype.itemsize for a in [*arrays, *shapes])
    buffers = buffers or {}
    used, extra = len(args), len(buffers) + len(after)

    def body(*refs):
        kernel(*refs[:used], *refs[used + extra :])

    return pl.pallas_call(
        body,
        grid=(1,),
        out_shape=tuple(shapes),
        in_specs=[*[SCALARS] * scalars, *map(spec_of, args[scalars:]), *[LEFT] * extra],
        out_specs=tuple(map(spec_of, outs)),
        input_output_aliases={used + j: o for j, o in enumerate(buffers)},
        scratch_shapes=scratch,
        compiler_params=pltpu.CompilerParams(vmem_limit_bytes=VMEM_LIMIT),
        cost_estimate=cost(name),
        name=name,
    )(*arrays, *buffers.values(), *after)


def prepare(array, bias, count):
    slots, share, _ = array.shape
    return run(prepare_kernel, [shaped(slots, share, count)], [array, bias], "prepare", 10**6)[0]


def prepare_grad(array, live, count, after=()):
    slots, share, _ = array.shape
    outs = [shaped(slots, share, count), shaped(8, share, dtype=F32)]
    return run(
        prepare_grad_kernel, outs, [live, array], "prepare", 10**6, after=after, scalars=1
    )


def attn_fwd(x, i, vec, w, bias, seq, after=()):
    slots, share, count = x[0].shape
    outs = [
        shaped(4 * share, count),
        shaped(3 * share // HDIM, HDIM, count),
        shaped(share, count),
        shaped(8, count, dtype=F32),
        shaped(8, count, dtype=F32),
    ]
    flops = 2 * count * 12 * share * share + 8 * count * count * 256
    return run(
        functools.partial(attn_fwd_kernel, seq), outs, [*[(a, i) for a in x], vec, w, bias],
        "attn_fwd", flops, after=after,
    )


def mlp_fwd(x, m, i, vec, w_out, up, up_bias, down, seq, buffers, after=()):
    slots, share, count = x[0].shape
    hidden = up.shape[0]
    outs = [
        shaped(4 * share, count),
        shaped(4 * share, count),
        shaped(hidden, count),
        shaped(hidden, count),
        (shaped(slots, share, count, dtype=F32), i),
        shaped(8, count, dtype=F32),
        (shaped(slots, share, count, dtype=F32), i),
        (shaped(slots, 2, share, count), i),
    ]
    flops = 2 * count * 4 * share * (4 * share + 2 * hidden)
    args = [*[(a, i) for a in x], *m, vec, w_out, up, up_bias, down]
    return run(
        functools.partial(mlp_fwd_kernel, seq), outs, args, "mlp_fwd", flops,
        after=after, buffers=buffers,
    )


def mlp_bwd(c, i, slope, down, up, after=()):
    _, share, count = c[0].shape
    hidden = up.shape[1]
    outs = [
        shaped(4 * share, count),
        shaped(hidden, count),
        shaped(2, share, count, dtype=F32),
        shaped(2, share, count),
        shaped(8, hidden, dtype=F32),
    ]
    flops = 2 * count * 4 * share * 2 * hidden
    args = [*[(a, i) for a in c], slope, down, up]
    return run(mlp_bwd_kernel, outs, args, "mlp_bwd", flops, after=after)


def attn_bwd(ng, cot, norm2, stats2, vec, w_out, qkv, lse, w, attn_in, seq, after=()):
    width, count = cot.shape
    share = width // 4
    outs = [
        shaped(width, count),
        shaped(share, count, dtype=F32),
        shaped(3 * share, count),
        shaped(share, count, dtype=F32),
        shaped(share, count, dtype=F32),
        shaped(2, share, count),
        shaped(8, count, dtype=F32),
        shaped(share, 8, dtype=F32),
        shaped(8, 3 * share, dtype=F32),
    ]
    flops = 2 * count * 16 * share * share + 20 * count * count * 256
    args = [*ng, cot, norm2, stats2, vec, w_out, qkv, lse, w, attn_in]
    scratch = (pltpu.VMEM((share // HDIM, HDIM, count), LOW),)
    return run(
        functools.partial(attn_bwd_kernel, seq), outs, args, "attn_bwd", flops, scratch, after
    )


def finish_grad(args, i, buffer, slots, seq):
    share = args[0].shape[0]
    outs = [(shaped(slots, share, seq), i), shaped(share, 8, dtype=F32)]
    buffers = {} if buffer is None else {0: buffer}

    def kernel(*refs):
        grad_kernel(*refs[:8], None, *refs[8:])

    return run(kernel, outs, args, "grad", 10**6, buffers=buffers)


def finish_out(live, base, came, across, seq):
    slots, share, count = base.shape
    return pl.pallas_call(
        out_kernel,
        grid=(slots,),
        out_shape=shaped(slots, share, seq),
        in_specs=[
            SCALARS,
            pl.BlockSpec((1, share, count), lambda i: (i, 0, 0)),
            pl.BlockSpec((1, 1, share, count), lambda i: (i, 0, 0, 0)),
            pl.BlockSpec((1, share, count), lambda i: (i, 0, 0)),
        ],
        out_specs=pl.BlockSpec((1, share, seq), lambda i: (i, 0, 0)),
        compiler_params=pltpu.CompilerParams(vmem_limit_bytes=VMEM_LIMIT),
        name="out",
    )(live, base, came, across)


def place(near, far, pos):
    count = 2 * len(near)
    rows, hidden = near[0].shape
    outs = [shaped(count, rows, hidden), shaped(hidden, count * rows)]
    placed, turned = run(place_kernel, outs, [pos, *near, far], "place", 10**6, scalars=1)
    return placed.reshape(count * rows, hidden), turned


def place_pair(near, far, cut, pos):
    count = 2 * len(near)
    rows, hidden = near[0].shape
    outs = [
        shaped(count, rows, cut),
        shaped(count, rows, hidden - cut),
        shaped(hidden - cut, count * rows),
    ]
    first, second, turned = run(
        place_pair_kernel, outs, [pos, *near, far], "place", 10**6, scalars=1
    )
    return first.reshape(count * rows, cut), second.reshape(count * rows, hidden - cut), turned


def join(near, far, after=()):
    rows, half = near.shape
    outs = [shaped(rows, 2 * half), shaped(half // 2, rows)]
    return run(join_kernel, outs, [near, far], "join", 10**6, after=after)


def weight_grad(a, b, order, after=()):
    width, count = a[0].shape
    share, hidden = width // 4, b[0].shape[0]
    slots = len(a)
    out = shaped(4, share, hidden)
    moved = sum(math.prod(v.shape) * 2 for v in [*a, *b, out])
    out = pl.pallas_call(
        lambda *refs: weight_grad_kernel(slots, *refs),
        out_shape=out,
        grid_spec=pltpu.PrefetchScalarGridSpec(
            num_scalar_prefetch=1,
            grid=(4,),
            in_specs=[
                *[pl.BlockSpec((share, count), lambda r, order: (r, 0)) for _ in a],
                *[pl.BlockSpec((hidden, count), lambda r, order: (0, 0)) for _ in b],
                *[pl.BlockSpec(memory_space=pl.ANY)] * len(after),
            ],
            out_specs=pl.BlockSpec((1, share, hidden), lambda r, order: (order[r], 0, 0)),
        ),
        compiler_params=pltpu.CompilerParams(vmem_limit_bytes=VMEM_LIMIT),
        cost_estimate=cost("weight_grad"),
        name="weight_grad",
    )(order, *a, *b, *after)
    return out.reshape(width, hidden)


def weight_part(a, b, after=()):
    width, count = a[0].shape
    share, hidden = width // 4, b[0].shape[0]
    return pl.pallas_call(
        lambda *refs: weight_part_kernel(len(a), *refs),
        out_shape=shaped(width, hidden, dtype=F32),
        grid=(4,),
        in_specs=[
            *[pl.BlockSpec((share, count), lambda r: (r, 0)) for _ in a],
            *[pl.BlockSpec((hidden, count), lambda r: (0, 0)) for _ in b],
            *[LEFT] * len(after),
        ],
        out_specs=pl.BlockSpec((share, hidden), lambda r: (r, 0)),
        compiler_params=pltpu.CompilerParams(vmem_limit_bytes=VMEM_LIMIT),
        cost_estimate=cost("weight_part"),
        name="weight_part",
    )(*a, *b, *after)


def weight_split(groups, order, odd, after=()):
    width, count = groups[0][0][0].shape
    share = width // 4
    args, specs, total = [], [], 0
    for a, b, start in groups:
        hidden = b[0].shape[0]
        args += [*a, *b]
        specs += [pl.BlockSpec((share, count), lambda r, order, odd: (r, 0)) for _ in a]
        specs += [pl.BlockSpec((hidden, count), lambda r, order, odd: (0, 0)) for _ in b]
        if start is not None:
            args.append(start)
            specs.append(pl.BlockSpec((share, hidden), lambda r, order, odd: (r, 0)))
        total += hidden
    outs = [shaped(4, share // 2, total, dtype=F32), shaped(4, share // 2, total)]
    counts = [len(g[0]) for g in groups]
    starts = [int(g[2] is not None) for g in groups]
    used = len(args) + 2

    def body(*refs):
        weight_split_kernel(counts, starts, *refs[:used], *refs[used + len(after) :])

    return pl.pallas_call(
        body,
        out_shape=outs,
        grid_spec=pltpu.PrefetchScalarGridSpec(
            num_scalar_prefetch=2,
            grid=(4,),
            in_specs=[*specs, *[LEFT] * len(after)],
            out_specs=[
                pl.BlockSpec((1, share // 2, total), lambda r, order, odd: (order[r], 0, 0))
            ]
            * 2,
        ),
        compiler_params=pltpu.CompilerParams(vmem_limit_bytes=VMEM_LIMIT),
        cost_estimate=cost("weight_grad"),
        name="weight_grad",
    )(order, odd, *args, *after)


def place_blocks_kernel(order, value, out, turned):
    for r in range(4):
        out[r] = value[order[r]]
    rows = out.shape[0] * out.shape[1]
    turned[...] = out[...].reshape(rows, out.shape[2]).T


def place_blocks(value, t, after=()):
    rows, hidden = value.shape
    order = jnp.stack([t ^ m for m in (0, 2, 1, 3)]).astype(jnp.int32)
    placed, turned = run(
        place_blocks_kernel,
        [shaped(4, rows // 4, hidden), shaped(hidden, rows)],
        [order, value.reshape(4, rows // 4, hidden)],
        "place",
        10**6,
        scalars=1,
        after=after,
    )
    return placed.reshape(rows, hidden), turned


def gate(values, after):
    values, after = list(values), list(after)
    left = pl.BlockSpec(memory_space=pl.ANY)
    return pl.pallas_call(
        lambda *refs: None,
        out_shape=[jax.ShapeDtypeStruct(v.shape, v.dtype) for v in values],
        in_specs=[left] * (len(values) + len(after)),
        out_specs=[left] * len(values),
        input_output_aliases={i: i for i in range(len(values))},
        cost_estimate=pl.CostEstimate(flops=0, bytes_accessed=0, transcendentals=0),
        name="gate",
    )(*values, *after)


def dp_swap(value, mask):
    size = lax.axis_size("dp")
    return lax.ppermute(value, "dp", [(i, i ^ mask) for i in range(size)])


def gather_dp_whole(shard, t):
    size = lax.axis_size("dp")
    value = lax.all_gather(shard, "dp", axis=0, tiled=True)
    if size != 8:
        value = rel_blocks(value, t)
        return value, value.T
    return place_blocks(value, t)


def gather_first(shard):
    return [shard, *[dp_swap(shard, m) for m in (2, 4, 6)]]


def shard_order(t):
    pos = []
    for m in range(8):
        k = lax.axis_index("dp") ^ m
        b = t ^ (k >> 1)
        pos.append((((b & 1) << 1) | (b >> 1)) * 2 + (k & 1))
    return jnp.stack(pos).astype(jnp.int32)


def gather_second(near, far, t):
    return place(near, far, shard_order(t))


def gather_pair(near, far, cut, t):
    return place_pair(near, far, cut, shard_order(t))


def weight_whole(a, b, t, after=()):
    order = jnp.stack([t ^ m for m in (0, 2, 1, 3)]).astype(jnp.int32)
    return weight_grad(a, b, order, after)


def scatter_rows(value):
    return lax.psum_scatter(value, "dp", scatter_dimension=0, tiled=True).astype(F32)


def scatter_whole(a, b, t, after=()):
    return scatter_rows(weight_whole(a, b, t, after))


def scatter_split(groups, t, after=()):
    order = jnp.stack([t ^ m for m in (0, 2, 1, 3)]).astype(jnp.int32)
    me = lax.axis_index("dp")
    return weight_split(groups, order ^ (me >> 1), (me & 1).reshape(1).astype(jnp.int32), after)


def scatter_first(keep, came):
    total = keep + came.astype(F32)
    return total[0], [total[j].astype(LOW) for j in (1, 2, 3)]


def scatter_second(sends):
    return [dp_swap(send, 2 * j) for j, send in zip((1, 2, 3), sends)]


def scatter_last(own, came):
    return own + came[0].astype(F32) + came[1].astype(F32) + came[2].astype(F32)


def sum_dp(value):
    size = lax.axis_size("dp")
    if size != 8:
        return lax.psum(value, "dp")
    value = value + dp_swap(value, 1)
    return sum((dp_swap(value, m) for m in (2, 4, 6)), value)


def columns(vectors, count=8):
    vectors = [*vectors, *[jnp.zeros_like(vectors[0])] * (count - len(vectors))]
    return jnp.stack(vectors, axis=1)


def local(
    images,
    image_count,
    attn_gain,
    attn_shift,
    query_weight,
    query_bias,
    key_weight,
    value_weight,
    value_bias,
    output_weight,
    output_bias,
    mlp_gain,
    mlp_shift,
    up_weight,
    up_bias,
    down_weight,
    down_bias,
    cotangent,
):
    images, cotangent = images.transpose(0, 2, 1), cotangent.transpose(0, 2, 1)
    slots, share, seq = images.shape
    t = lax.axis_index("tensor")
    count = -(-seq // TILE) * TILE
    zero = jnp.zeros_like(output_bias)
    gains = [rel_blocks(a, t) for a in (attn_gain, attn_shift, mlp_gain, mlp_shift)]
    down_rows = jnp.concatenate([down_bias, zero, zero, zero])
    vec = columns([gains[0], gains[1], gains[1], gains[2], gains[3], down_rows])
    vec_own = vec[:share]
    qkv_bias = columns([jnp.concatenate([query_bias, zero, value_bias])])
    up_b = columns([up_bias])
    live = (jnp.arange(slots) < image_count[0]).astype(F32)

    fast = lax.axis_size("dp") == 8
    qkv_shard = jnp.concatenate([query_weight, key_weight, value_weight], axis=1)
    out_t = output_weight.T
    out_shard = jnp.concatenate([out_t, y_swap(out_t)], axis=1)
    up_value = lax.all_gather(up_weight, "dp", axis=0, tiled=True)
    x_own = prepare(images, columns([output_bias]), count)
    x_send, qkv_shard = gate([x_own, qkv_shard], [out_shard])
    x_far, x_across = core_swap(x_send), y_swap(x_send)
    if fast:
        near = gather_first(qkv_shard)
        cot_own, cot_sums = prepare_grad(cotangent, live, count, [x_own])
        out_shard = jnp.concatenate([out_shard, down_weight.T], axis=1)
        *near[1:], out_shard = gate([*near[1:], out_shard], [x_far, cot_sums])
        near_stack = jnp.stack(near)
        far = dp_swap(near_stack, 1)
        out_near = gather_first(out_shard)
        (x_across,) = gate([x_across], [near_stack])
        x_wide = core_swap(x_across)
        (cot_send,) = gate([cot_own], [x_wide])
        cot_across = y_swap(cot_send)
        qkv_w, qkv_t = gather_second(near, far, t)
    else:
        x_wide = core_swap(x_across)
        cot_own, cot_sums = prepare_grad(cotangent, live, count, [x_own])
        cot_across = y_swap(cot_own)
        qkv_w, qkv_t = gather_dp_whole(qkv_shard, t)
        o_half, _ = gather_dp_whole(out_shard, t)
        down_t, down_w = gather_dp_whole(down_weight.T, t)
        up_w, up_t = gather_dp_whole(up_weight, t)
    x = [x_own, x_across, x_far, x_wide]

    def forward(i, after):
        fwd.append(attn_fwd(x, i, vec, qkv_t, qkv_bias, seq, after))
        mixes.append([fwd[i][2], y_swap(fwd[i][2])])

    def widen(i):
        mixes[i].extend([core_swap(mixes[i][0]), core_swap(mixes[i][1])])

    fwd, mixes = [], []
    forward(0, [cot_sums])
    if fast:
        out_near[1:] = gate(out_near[1:], [fwd[0][4]])
        out_stack = jnp.stack(out_near)
        out_far = dp_swap(out_stack, 1)
        forward(1, [fwd[0][4], out_stack])
    else:
        forward(1, [fwd[0][4]])
    (cot_across,) = gate([cot_across], [fwd[1][4]])
    cot_far, cot_wide = core_swap(cot_own), core_swap(cot_across)
    forward(2, [fwd[1][4], cot_far])
    mixes[0][1], mixes[1][1] = gate([mixes[0][1], mixes[1][1]], [fwd[2][4], cot_wide])
    widen(0)
    widen(1)
    if fast:
        up_w, up_t = place_blocks(up_value, t, [cot_far, cot_wide])
    widen(2)
    if fast:
        (out_far,) = gate([out_far], [v for m in mixes for v in m])
        o_half, down_t, down_w = gather_pair(out_near, out_far, 2 * share, t)
    o_full, o_mine = join(o_half, core_swap(o_half))
    cot = [cot_own, cot_across, cot_far, cot_wide]

    mlp, back, ends, norm2_grad = [], [], [], []

    def mlp_forward(i, after):
        buffers = {j: mlp[i - 1][j] for j in (4, 6, 7)} if i else {}
        mlp.append(mlp_fwd(x, mixes[i], i, vec, o_full, up_t, up_b, down_t, seq, buffers, after))

    def mlp_back(i, after):
        back.append(mlp_bwd(cot, i, mlp[i][3], down_w, up_w, after))
        half = back[i][2] + core_swap(back[i][3]).astype(F32)
        send = half[::-1].astype(LOW)
        norm2_grad.append([half, y_swap(send)])
        return send

    def norm2_wide(i):
        half, across = norm2_grad[i]
        both = (half + across.astype(F32)).astype(LOW)
        norm2_grad[i].append(core_swap(both))
        return both

    def attention_back(i, after):
        attn_in, qkv, _, stats1, lse = fwd[i]
        norm2, stats2 = mlp[i][1], mlp[i][5]
        ends.append(
            attn_bwd(
                norm2_grad[i], back[i][0], norm2, stats2, vec, o_mine, qkv, lse, qkv_w, attn_in,
                seq, after,
            )
        )

    mlp_forward(0, [])
    send = mlp_back(0, [mlp[0][5]])
    mlp_forward(1, [send])
    norm2_grad[0][1], *_ = gate([norm2_grad[0][1]], [mlp[1][5]])
    both = norm2_wide(0)
    send = mlp_back(1, [both])
    mlp_forward(2, [send, norm2_grad[0][2]])
    norm2_grad[1][1], mlp_send = gate([norm2_grad[1][1], mlp[2][7]], [mlp[2][5]])
    both = norm2_wide(1)
    mlp_came = core_swap(mlp_send)
    send = mlp_back(2, [both])
    base, keep = mlp[2][4], mlp[2][6]
    (mlp_came,) = gate([mlp_came], [send])
    out_send = (keep + mlp_came[:, 1].astype(F32)).astype(LOW)

    up_rows = weight_whole(
        [m[0] for m in mlp], [b[1] for b in back], t, [send, norm2_grad[1][2], out_send]
    )
    up_grad = scatter_rows(up_rows)
    terms = [b[0] for b in back], [m[2] for m in mlp]
    if fast:
        down_keep, last = scatter_split([(*terms, None)], t, [up_rows])
        down_x = dp_swap(last, 1)
    else:
        last = weight_whole(*terms, t, [up_rows])
        down_grad = scatter_rows(last)
    norm2_grad[2][1], out_send = gate([norm2_grad[2][1], out_send], [last])
    both = norm2_wide(2)
    (out_send,) = gate([out_send], [both])
    out_across = y_swap(out_send)
    attention_back(0, [both, last])
    came = [core_swap(ends[0][5])]
    attention_back(1, [ends[0][-1], norm2_grad[2][2]])
    if fast:
        (down_x,) = gate([down_x], [ends[1][-1]])
        down_own, down_sends = scatter_first(down_keep, down_x)
        down_came = scatter_second(down_sends)
    came.append(core_swap(*gate([ends[1][5]], [came[0], out_across])))
    send = jnp.stack([(ends[i][4] + came[i][1].astype(F32)).astype(LOW) for i in (0, 1)])
    across = [y_swap(send)]
    qkv_part = weight_part([f[0] for f in fwd[:2]], [e[2] for e in ends], [send])
    out_part = weight_part([e[0] for e in ends], [f[2] for f in fwd[:2]], [send])
    attention_back(2, [qkv_part, out_part, up_grad])
    e = ends[2]
    stats = jnp.concatenate([v[6] for v in ends])
    if fast:
        keep_a, send_a = scatter_split([([fwd[2][0]], [e[2]], qkv_part)], t, [e[-1]])
        x_a = dp_swap(send_a, 1)
        part, stats, *down_came = gate([e[5], stats, *down_came], [send_a])
        down_grad = scatter_last(down_own, down_came)
    else:
        qkv_grad = scatter_whole([f[0] for f in fwd], [v[2] for v in ends], t)
        out_grad = scatter_whole([v[0] for v in ends], [f[2] for f in fwd], t)
        part = e[5]
    came_last = core_swap(part)
    came.append(came_last)
    send = (e[4] + came_last[1].astype(F32)).astype(LOW)[None]
    stats = stats + core_swap(stats)
    across.append(y_swap(send))
    stats = stats + y_swap(stats)
    if fast:
        keep_b, send_b = scatter_split([([e[0]], [fwd[2][2]], out_part)], t, [send])
        x_b = dp_swap(send_b, 1)
        (out_across,) = gate([out_across], [send_b])
        own_a, sends_a = scatter_first(keep_a, x_a)
        came_a = scatter_second(sends_a)
        *came_a, x_b = gate([*came_a, x_b], [send_b])
        own_b, sends_b = scatter_first(keep_b, x_b)
        came_b = scatter_second(sends_b)
        qkv_grad = scatter_last(own_a, came_a)
        out_grad = scatter_last(own_b, came_b)
    out_buffer = finish_out(live, base, mlp_came, out_across, seq)
    grad_buffer, sums = None, None
    for i in range(slots):
        grad_buffer, grad_sums = finish_grad(
            [ends[i][1], ends[i][3], came[i], (across[i // 2], i % 2), (x_own, i), fwd[i][3],
             stats[8 * i : 8 * i + 8], vec_own],
            i, grad_buffer, slots, seq,
        )
        now = (grad_sums, ends[i][7], ends[i][8], back[i][-1])
        sums = now if sums is None else jax.tree.map(jnp.add, sums, now)
    down_grad, out_grad = down_grad.T, out_grad.T
    sums = (*sums, cot_sums)
    sizes = [2 * share, 3 * share, 3 * share, up_bias.shape[0], share]
    small = jnp.concatenate(
        [
            sums[0][:, :2].T.reshape(-1),
            sums[1][:, :3].T.reshape(-1),
            sums[2][0],
            sums[3][0],
            sums[4][0],
        ]
    )
    if fast:
        (small,) = gate([small], [x_b])
    small = sum_dp(small)
    parts, at = [], 0
    for size in sizes:
        parts.append(small[at : at + size])
        at += size
    grad_sums, own_sums = parts[0].reshape(2, share), parts[1].reshape(3, share)
    qkv_sums, up_sum, cot_sum = parts[2:]
    return (
        out_buffer.transpose(0, 2, 1),
        grad_buffer.transpose(0, 2, 1),
        grad_sums[0],
        grad_sums[1],
        qkv_grad[:, :share],
        qkv_sums[:share],
        qkv_grad[:, share : 2 * share],
        qkv_grad[:, 2 * share :],
        qkv_sums[2 * share :],
        out_grad,
        own_sums[0],
        own_sums[1],
        own_sums[2],
        up_grad,
        up_sum,
        down_grad,
        cot_sum,
    )


def solution(mesh):
    in_specs = (
        P("dp", None, "tensor"),
        P("dp"),
        P(),
        P(),
        P("dp", "tensor"),
        P("tensor"),
        P("dp", "tensor"),
        P("dp", "tensor"),
        P("tensor"),
        P("tensor", "dp"),
        P("tensor"),
        P(),
        P(),
        P("dp", "tensor"),
        P("tensor"),
        P("tensor", "dp"),
        P("tensor"),
        P("dp", None, "tensor"),
    )
    out_specs = (
        P("dp", None, "tensor"),
        P("dp", None, "tensor"),
        P("tensor"),
        P("tensor"),
        P("dp", "tensor"),
        P("tensor"),
        P("dp", "tensor"),
        P("dp", "tensor"),
        P("tensor"),
        P("tensor", "dp"),
        P("tensor"),
        P("tensor"),
        P("tensor"),
        P("dp", "tensor"),
        P("tensor"),
        P("tensor", "dp"),
        P("tensor"),
    )
    return jax.shard_map(local, mesh=mesh, in_specs=in_specs, out_specs=out_specs, check_vma=False)
```

```python
import functools
import math

import jax
import jax.numpy as jnp
from jax import lax
from jax.experimental import pallas as pl
from jax.experimental.pallas import tpu as pltpu
from jax.sharding import PartitionSpec as P

HDIM = 72
EPSILON = 1e-06
LOG2E = 1.4426950408889634
MASKED = -1e30
GELU_A = math.sqrt(2.0 / math.pi)
GELU_B = 0.044715
TILE = 256
VMEM_LIMIT = 56 * 2**20
F32 = jnp.float32
LOW = jnp.bfloat16
Y_SWAP = [(0, 2), (2, 0), (1, 3), (3, 1)]
CORE_SWAP = [(0, 1), (1, 0), (2, 3), (3, 2)]


def y_swap(value):
    return lax.ppermute(value, "tensor", Y_SWAP)


def core_swap(value):
    return lax.ppermute(value, "tensor", CORE_SWAP)


def dot_nn(a, b):
    return lax.dot_general(a, b, (((1,), (0,)), ((), ())), preferred_element_type=F32)


def dot_nt(a, b):
    return lax.dot_general(a, b, (((1,), (1,)), ((), ())), preferred_element_type=F32)


def dot_tn(a, b):
    return lax.dot_general(a, b, (((0,), (0,)), ((), ())), preferred_element_type=F32)


def rel_blocks(value, t):
    width = value.shape[0] // 4
    return jnp.concatenate(
        [lax.dynamic_slice_in_dim(value, (t ^ m) * width, width, 0) for m in (0, 2, 1, 3)], axis=0
    )


def rows4(a, b, c, d):
    return jnp.concatenate([a, b, c, d], axis=0)


def lanes(count):
    return [slice(at, at + TILE) for at in range(0, count, TILE)]


def column(sums):
    pad = jnp.zeros((sums[0].shape[0], 8 - len(sums)), F32)
    return jnp.concatenate([*sums, pad], axis=1)


def prepare_kernel(x, bias, out):
    slots, share, seq = x.shape
    high = bias[:, 0:1].astype(LOW)
    rest = bias[:, 0:1] - high.astype(F32)
    mid = rest.astype(LOW)
    for i in range(slots):
        out[i] = jnp.zeros(out.shape[1:], LOW)
        out[i, :, :seq] = x[i]
        out[i, :, seq : seq + 1] = high
        out[i, :, seq + 1 : seq + 2] = mid
        out[i, :, seq + 2 : seq + 3] = (rest - mid.astype(F32)).astype(LOW)


def prepare_grad_kernel(live, x, out, sums):
    slots, share, seq = x.shape
    total = 0.0
    for i in range(slots):
        out[i] = jnp.zeros(out.shape[1:], LOW)
        out[i, :, :seq] = (x[i].astype(F32) * live[i]).astype(LOW)
        total = total + dot_nt(jnp.ones((8, out.shape[2]), LOW), out[i])
    sums[...] = total


def place_pair_kernel(pos, *refs):
    count = len(refs) - 4
    far, first, second, turned = refs[count:]
    cut = first.shape[2]
    for m in range(count):
        first[pos[2 * m]] = refs[m][:, :cut]
        first[pos[2 * m + 1]] = far[m, :, :cut]
        second[pos[2 * m]] = refs[m][:, cut:]
        second[pos[2 * m + 1]] = far[m, :, cut:]
    rows = second.shape[0] * second.shape[1]
    turned[...] = second[...].reshape(rows, second.shape[2]).T


def place_kernel(pos, *refs):
    count = len(refs) - 3
    far, out, turned = refs[count:]
    for m in range(count):
        out[pos[2 * m]] = refs[m][...]
        out[pos[2 * m + 1]] = far[m]
    rows = out.shape[0] * out.shape[1]
    turned[...] = out[...].reshape(rows, out.shape[2]).T


def join_kernel(near, far, out, turned):
    rows, half = near.shape
    out[:, :half] = near[...]
    out[: rows // 2, half:] = far[rows // 2 :]
    out[rows // 2 :, half:] = far[: rows // 2]
    turned[...] = near[:, : half // 2].T


def attn_fwd_kernel(seq, xo, xy, xc, xd, vec, w, bias, attn_in, qkv, mixed, stats, lse):
    share, count = xo.shape
    heads = share // HDIM
    gain, shift = vec[:, 0:1], vec[:, 1:2]
    for at in lanes(count):
        x = rows4(xo[:, at], xy[:, at], xc[:, at], xd[:, at]).astype(F32)
        mean = jnp.mean(x, axis=0, keepdims=True)
        centred = x - mean
        inverse = lax.rsqrt(jnp.mean(centred * centred, axis=0, keepdims=True) + EPSILON)
        low = (centred * inverse * gain + shift).astype(LOW)
        attn_in[:, at] = low
        stats[0:1, at] = mean
        stats[1:2, at] = inverse
        part = dot_nn(w[...], low) + bias[:, 0:1]
        for i in range(3 * heads):
            qkv[i, :, at] = part[i * HDIM : (i + 1) * HDIM].astype(LOW)
    c = LOG2E / math.sqrt(HDIM)
    mask = lax.broadcasted_iota(jnp.int32, (count, 1), 0) < seq
    out = []
    for h in range(heads):
        q, k, v = qkv[h], qkv[heads + h], qkv[2 * heads + h]
        s = jnp.where(mask, dot_tn(k, q), MASKED)
        top = jnp.max(s, axis=0, keepdims=True)
        e = jnp.exp2((s - top) * c)
        total = jnp.sum(e, axis=0, keepdims=True)
        lse[h : h + 1, :] = top * c + jnp.log2(total)
        out.append(dot_nn(v, e.astype(LOW)) * (1.0 / total))
    mixed[...] = jnp.concatenate(out, axis=0).astype(LOW)


def mlp_fwd_kernel(
    seq, xo, xy, xc, xd, mo, my, mc, md, vec, w_out, up, up_bias, down,
    mlp_in, norm2, activ, slope, base, stats, keep, send,
):
    share, count = xo.shape
    gain, shift = vec[:, 3:4], vec[:, 4:5]
    tail = rows4(xo[:, seq:], xy[:, seq:], xc[:, seq:], xd[:, seq:]).astype(F32)
    o_bias = tail[:, 0:1] + tail[:, 1:2] + tail[:, 2:3]
    for at in lanes(count):
        mixed = rows4(mo[:, at], my[:, at], mc[:, at], md[:, at])
        x = rows4(xo[:, at], xy[:, at], xc[:, at], xd[:, at]).astype(F32)
        hidden = x + dot_nn(w_out[...], mixed) + o_bias
        mean = jnp.mean(hidden, axis=0, keepdims=True)
        centred = hidden - mean
        inverse = lax.rsqrt(jnp.mean(centred * centred, axis=0, keepdims=True) + EPSILON)
        normed = centred * inverse
        stats[0:1, at] = inverse
        norm2[:, at] = normed.astype(LOW)
        low = (normed * gain + shift).astype(LOW)
        mlp_in[:, at] = low
        v = dot_nn(up[...], low) + up_bias[:, 0:1]
        square = v * v
        tanh = jnp.tanh(v * (GELU_A + GELU_A * GELU_B * square))
        gate = 0.5 + 0.5 * tanh
        act = (v * gate).astype(LOW)
        activ[:, at] = act
        slope[:, at] = (
            gate + v * (0.5 - 0.5 * tanh * tanh) * (GELU_A + 3.0 * GELU_A * GELU_B * square)
        ).astype(LOW)
        part = dot_nn(down[...], act)
        base[:, at] = hidden[:share] + part[:share] + vec[:share, 5:6]
        keep[:, at] = part[share : 2 * share]
        send[0, :, at] = part[2 * share : 3 * share].astype(LOW)
        send[1, :, at] = part[3 * share :].astype(LOW)


def mlp_bwd_kernel(co, cy, cc, cd, slope, down, up, cot, pre_grad, keep, send, sums):
    share, count = co.shape
    for at in lanes(count):
        c = rows4(co[:, at], cy[:, at], cc[:, at], cd[:, at])
        cot[:, at] = c
        low = (dot_nn(down[...], c) * slope[:, at].astype(F32)).astype(LOW)
        pre_grad[:, at] = low
        part = dot_nn(up[...], low)
        keep[0, :, at] = part[:share]
        keep[1, :, at] = part[share : 2 * share]
        send[0, :, at] = part[2 * share : 3 * share].astype(LOW)
        send[1, :, at] = part[3 * share :].astype(LOW)
    sums[...] = dot_nt(jnp.ones((8, count), LOW), pre_grad[...])


def attn_bwd_kernel(
    seq, half, across, far, cot, norm2, stats2, vec, w_out, qkv, lse, w, attn_in,
    branch, h_grad, dqkv, keep_o, keep_y, send, stats, sums_own, sums_qkv,
    dmix,
):
    width, count = cot.shape
    share = width // 4
    heads = share // HDIM
    gain2 = vec[:, 3:4]
    sums = [0.0, 0.0, 0.0]
    for at in lanes(count):
        near = half[:, :, at] + across[:, :, at].astype(F32)
        ng = rows4(near[0], near[1], far[0, :, at].astype(F32), far[1, :, at].astype(F32))
        n2 = norm2[:, at].astype(F32)
        g = ng * gain2
        first = jnp.mean(g, axis=0, keepdims=True)
        second = jnp.mean(g * n2, axis=0, keepdims=True)
        hg = cot[:, at].astype(F32) + stats2[0:1, at] * (g - first - n2 * second)
        h_grad[:, at] = hg[:share]
        low = hg.astype(LOW)
        branch[:, at] = low
        dm = dot_nn(w_out[...], low)
        for h in range(heads):
            dmix[h, :, at] = dm[h * HDIM : (h + 1) * HDIM].astype(LOW)
        own = ng[:share]
        now = [hg[:share], own * n2[:share], own]
        sums = [a + jnp.sum(b, axis=1, keepdims=True) for a, b in zip(sums, now)]
    sums_own[...] = column(sums)
    scale = 1.0 / math.sqrt(HDIM)
    c = LOG2E * scale
    mask = lax.broadcasted_iota(jnp.int32, (count, 1), 0) < seq
    dq, dk, dv = [], [], []
    for h in range(heads):
        q, k, v, dm = qkv[h], qkv[heads + h], qkv[2 * heads + h], dmix[h]
        p = jnp.where(mask, jnp.exp2(dot_tn(k, q) * c - lse[h : h + 1, :]), 0.0)
        dp = dot_tn(v, dm)
        delta = jnp.sum(p * dp, axis=0, keepdims=True)
        ds = (p * (dp - delta)).astype(LOW)
        dq.append(dot_nn(k, ds) * scale)
        dk.append(dot_nt(q, ds) * scale)
        dv.append(dot_nt(dm, p.astype(LOW)))
    for j, part in enumerate((dq, dk, dv)):
        dqkv[j * share : (j + 1) * share, :] = jnp.concatenate(part, axis=0).astype(LOW)
    gain1, shift1 = vec[:, 0:1], vec[:, 1:2]
    for at in lanes(count):
        part = dot_nn(w[...], dqkv[:, at])
        keep_o[:, at] = part[:share]
        keep_y[:, at] = part[share : 2 * share]
        send[0, :, at] = part[2 * share : 3 * share].astype(LOW)
        send[1, :, at] = part[3 * share :].astype(LOW)
        stats[0:1, at] = jnp.sum(part * gain1, axis=0, keepdims=True)
        stats[1:2, at] = jnp.sum(part * (attn_in[:, at].astype(F32) - shift1), axis=0, keepdims=True)
    sums_qkv[...] = dot_nt(jnp.ones((8, count), LOW), dqkv[...])


def out_kernel(live, base, came, across, out):
    seq = out.shape[2]
    rows = base[0] + came[0, 0].astype(F32) + across[0].astype(F32)
    out[0] = (rows * live[pl.program_id(0)])[:, :seq].astype(LOW)


def grad_kernel(h_grad, keep, came, across, x_own, stats1, stats, vec, _, out, sums):
    share, seq = out.shape
    ng = keep[...] + came[0].astype(F32) + across[...].astype(F32)
    inverse = stats1[1:2, :]
    n1 = (x_own[...].astype(F32) - stats1[0:1, :]) * inverse
    mean = stats[...] * (1.0 / (4 * share))
    rows = h_grad[...] + inverse * (ng * vec[:, 0:1] - mean[0:1] - n1 * mean[1:2])
    out[...] = rows[:, :seq].astype(LOW)
    sums[...] = column(
        [jnp.sum(ng * n1, axis=1, keepdims=True), jnp.sum(ng, axis=1, keepdims=True)]
    )


def weight_grad_kernel(count, *refs):
    a, b, out = refs[1 : count + 1], refs[count + 1 : 2 * count + 1], refs[-1]
    total = dot_nt(a[0][...], b[0][...])
    for i in range(1, count):
        total = total + dot_nt(a[i][...], b[i][...])
    out[0] = total.astype(LOW)


def row_sum(pairs, start):
    total = None if start is None else start[...]
    for a, b in pairs:
        part = dot_nt(a[...], b[...])
        total = part if total is None else total + part
    return total


def weight_part_kernel(count, *refs):
    refs[-1][...] = row_sum(list(zip(refs[:count], refs[count : 2 * count])), None)


def weight_split_kernel(counts, starts, *refs):
    odd, refs = refs[1][0] == 1, list(refs[2:])
    keep, send = refs[-2:]
    at = 0
    for count, start in zip(counts, starts):
        pairs = list(zip(refs[:count], refs[count : 2 * count]))
        total = row_sum(pairs, refs[2 * count] if start else None)
        refs = refs[2 * count + start :]
        half = total.shape[0] // 2
        top, low = total[:half], total[half:]
        to = at + total.shape[1]
        keep[0, :, at:to] = jnp.where(odd, low, top)
        send[0, :, at:to] = jnp.where(odd, top, low).astype(LOW)
        at = to


TIMES = {
    "prepare": 2.6,
    "place": 4.0,
    "join": 4.0,
    "attn_fwd": 10.0,
    "mlp_fwd": 19.5,
    "mlp_bwd": 11.0,
    "attn_bwd": 17.7,
    "weight_grad": 12.4,
    "weight_part": 7.0,
    "grad": 3.3,
}
RATE = 2e8


def cost(name):
    return pl.CostEstimate(
        flops=int(TIMES[name] * RATE), bytes_accessed=0, transcendentals=0
    )


def shaped(*dims, dtype=LOW):
    return jax.ShapeDtypeStruct(dims, dtype)


def spec_of(array):
    if isinstance(array, tuple):
        array, i = array
        zeros = (0,) * (len(array.shape) - 1)
        return pl.BlockSpec(
            (None, *array.shape[1:]), lambda _: (i, *zeros), pipeline_mode=pl.Buffered(1)
        )
    zeros = (0,) * len(array.shape)
    return pl.BlockSpec(array.shape, lambda _: zeros, pipeline_mode=pl.Buffered(1))


SCALARS = pl.BlockSpec(memory_space=pltpu.SMEM)
LEFT = pl.BlockSpec(memory_space=pl.ANY)


def array_of(array):
    return array[0] if isinstance(array, tuple) else array


def run(kernel, outs, args, name, flops, scratch=(), after=(), scalars=0, buffers=None):
    arrays = [array_of(a) for a in args]
    shapes = [array_of(o) for o in outs]
    moved = sum(math.prod(a.shape) * a.dtype.itemsize for a in [*arrays, *shapes])
    buffers = buffers or {}
    used, extra = len(args), len(buffers) + len(after)

    def body(*refs):
        kernel(*refs[:used], *refs[used + extra :])

    return pl.pallas_call(
        body,
        grid=(1,),
        out_shape=tuple(shapes),
        in_specs=[*[SCALARS] * scalars, *map(spec_of, args[scalars:]), *[LEFT] * extra],
        out_specs=tuple(map(spec_of, outs)),
        input_output_aliases={used + j: o for j, o in enumerate(buffers)},
        scratch_shapes=scratch,
        compiler_params=pltpu.CompilerParams(vmem_limit_bytes=VMEM_LIMIT),
        cost_estimate=cost(name),
        name=name,
    )(*arrays, *buffers.values(), *after)


def prepare(array, bias, count):
    slots, share, _ = array.shape
    return run(prepare_kernel, [shaped(slots, share, count)], [array, bias], "prepare", 10**6)[0]


def prepare_grad(array, live, count, after=()):
    slots, share, _ = array.shape
    outs = [shaped(slots, share, count), shaped(8, share, dtype=F32)]
    return run(
        prepare_grad_kernel, outs, [live, array], "prepare", 10**6, after=after, scalars=1
    )


def attn_fwd(x, i, vec, w, bias, seq, after=()):
    slots, share, count = x[0].shape
    outs = [
        shaped(4 * share, count),
        shaped(3 * share // HDIM, HDIM, count),
        shaped(share, count),
        shaped(8, count, dtype=F32),
        shaped(8, count, dtype=F32),
    ]
    flops = 2 * count * 12 * share * share + 8 * count * count * 256
    return run(
        functools.partial(attn_fwd_kernel, seq), outs, [*[(a, i) for a in x], vec, w, bias],
        "attn_fwd", flops, after=after,
    )


def mlp_fwd(x, m, i, vec, w_out, up, up_bias, down, seq, buffers, after=()):
    slots, share, count = x[0].shape
    hidden = up.shape[0]
    outs = [
        shaped(4 * share, count),
        shaped(4 * share, count),
        shaped(hidden, count),
        shaped(hidden, count),
        (shaped(slots, share, count, dtype=F32), i),
        shaped(8, count, dtype=F32),
        (shaped(slots, share, count, dtype=F32), i),
        (shaped(slots, 2, share, count), i),
    ]
    flops = 2 * count * 4 * share * (4 * share + 2 * hidden)
    args = [*[(a, i) for a in x], *m, vec, w_out, up, up_bias, down]
    return run(
        functools.partial(mlp_fwd_kernel, seq), outs, args, "mlp_fwd", flops,
        after=after, buffers=buffers,
    )


def mlp_bwd(c, i, slope, down, up, after=()):
    _, share, count = c[0].shape
    hidden = up.shape[1]
    outs = [
        shaped(4 * share, count),
        shaped(hidden, count),
        shaped(2, share, count, dtype=F32),
        shaped(2, share, count),
        shaped(8, hidden, dtype=F32),
    ]
    flops = 2 * count * 4 * share * 2 * hidden
    args = [*[(a, i) for a in c], slope, down, up]
    return run(mlp_bwd_kernel, outs, args, "mlp_bwd", flops, after=after)


def attn_bwd(ng, cot, norm2, stats2, vec, w_out, qkv, lse, w, attn_in, seq, after=()):
    width, count = cot.shape
    share = width // 4
    outs = [
        shaped(width, count),
        shaped(share, count, dtype=F32),
        shaped(3 * share, count),
        shaped(share, count, dtype=F32),
        shaped(share, count, dtype=F32),
        shaped(2, share, count),
        shaped(8, count, dtype=F32),
        shaped(share, 8, dtype=F32),
        shaped(8, 3 * share, dtype=F32),
    ]
    flops = 2 * count * 16 * share * share + 20 * count * count * 256
    args = [*ng, cot, norm2, stats2, vec, w_out, qkv, lse, w, attn_in]
    scratch = (pltpu.VMEM((share // HDIM, HDIM, count), LOW),)
    return run(
        functools.partial(attn_bwd_kernel, seq), outs, args, "attn_bwd", flops, scratch, after
    )


def finish_grad(args, i, buffer, slots, seq):
    share = args[0].shape[0]
    outs = [(shaped(slots, share, seq), i), shaped(share, 8, dtype=F32)]
    buffers = {} if buffer is None else {0: buffer}

    def kernel(*refs):
        grad_kernel(*refs[:8], None, *refs[8:])

    return run(kernel, outs, args, "grad", 10**6, buffers=buffers)


def finish_out(live, base, came, across, seq):
    slots, share, count = base.shape
    return pl.pallas_call(
        out_kernel,
        grid=(slots,),
        out_shape=shaped(slots, share, seq),
        in_specs=[
            SCALARS,
            pl.BlockSpec((1, share, count), lambda i: (i, 0, 0)),
            pl.BlockSpec((1, 1, share, count), lambda i: (i, 0, 0, 0)),
            pl.BlockSpec((1, share, count), lambda i: (i, 0, 0)),
        ],
        out_specs=pl.BlockSpec((1, share, seq), lambda i: (i, 0, 0)),
        compiler_params=pltpu.CompilerParams(vmem_limit_bytes=VMEM_LIMIT),
        name="out",
    )(live, base, came, across)


def place(near, far, pos):
    count = 2 * len(near)
    rows, hidden = near[0].shape
    outs = [shaped(count, rows, hidden), shaped(hidden, count * rows)]
    placed, turned = run(place_kernel, outs, [pos, *near, far], "place", 10**6, scalars=1)
    return placed.reshape(count * rows, hidden), turned


def place_pair(near, far, cut, pos):
    count = 2 * len(near)
    rows, hidden = near[0].shape
    outs = [
        shaped(count, rows, cut),
        shaped(count, rows, hidden - cut),
        shaped(hidden - cut, count * rows),
    ]
    first, second, turned = run(
        place_pair_kernel, outs, [pos, *near, far], "place", 10**6, scalars=1
    )
    return first.reshape(count * rows, cut), second.reshape(count * rows, hidden - cut), turned


def join(near, far, after=()):
    rows, half = near.shape
    outs = [shaped(rows, 2 * half), shaped(half // 2, rows)]
    return run(join_kernel, outs, [near, far], "join", 10**6, after=after)


def weight_grad(a, b, order, after=()):
    width, count = a[0].shape
    share, hidden = width // 4, b[0].shape[0]
    slots = len(a)
    out = shaped(4, share, hidden)
    moved = sum(math.prod(v.shape) * 2 for v in [*a, *b, out])
    out = pl.pallas_call(
        lambda *refs: weight_grad_kernel(slots, *refs),
        out_shape=out,
        grid_spec=pltpu.PrefetchScalarGridSpec(
            num_scalar_prefetch=1,
            grid=(4,),
            in_specs=[
                *[pl.BlockSpec((share, count), lambda r, order: (r, 0)) for _ in a],
                *[pl.BlockSpec((hidden, count), lambda r, order: (0, 0)) for _ in b],
                *[pl.BlockSpec(memory_space=pl.ANY)] * len(after),
            ],
            out_specs=pl.BlockSpec((1, share, hidden), lambda r, order: (order[r], 0, 0)),
        ),
        compiler_params=pltpu.CompilerParams(vmem_limit_bytes=VMEM_LIMIT),
        cost_estimate=cost("weight_grad"),
        name="weight_grad",
    )(order, *a, *b, *after)
    return out.reshape(width, hidden)


def weight_part(a, b, after=()):
    width, count = a[0].shape
    share, hidden = width // 4, b[0].shape[0]
    return pl.pallas_call(
        lambda *refs: weight_part_kernel(len(a), *refs),
        out_shape=shaped(width, hidden, dtype=F32),
        grid=(4,),
        in_specs=[
            *[pl.BlockSpec((share, count), lambda r: (r, 0)) for _ in a],
            *[pl.BlockSpec((hidden, count), lambda r: (0, 0)) for _ in b],
            *[LEFT] * len(after),
        ],
        out_specs=pl.BlockSpec((share, hidden), lambda r: (r, 0)),
        compiler_params=pltpu.CompilerParams(vmem_limit_bytes=VMEM_LIMIT),
        cost_estimate=cost("weight_part"),
        name="weight_part",
    )(*a, *b, *after)


def weight_split(groups, order, odd, after=()):
    width, count = groups[0][0][0].shape
    share = width // 4
    args, specs, total = [], [], 0
    for a, b, start in groups:
        hidden = b[0].shape[0]
        args += [*a, *b]
        specs += [pl.BlockSpec((share, count), lambda r, order, odd: (r, 0)) for _ in a]
        specs += [pl.BlockSpec((hidden, count), lambda r, order, odd: (0, 0)) for _ in b]
        if start is not None:
            args.append(start)
            specs.append(pl.BlockSpec((share, hidden), lambda r, order, odd: (r, 0)))
        total += hidden
    outs = [shaped(4, share // 2, total, dtype=F32), shaped(4, share // 2, total)]
    counts = [len(g[0]) for g in groups]
    starts = [int(g[2] is not None) for g in groups]
    used = len(args) + 2

    def body(*refs):
        weight_split_kernel(counts, starts, *refs[:used], *refs[used + len(after) :])

    return pl.pallas_call(
        body,
        out_shape=outs,
        grid_spec=pltpu.PrefetchScalarGridSpec(
            num_scalar_prefetch=2,
            grid=(4,),
            in_specs=[*specs, *[LEFT] * len(after)],
            out_specs=[
                pl.BlockSpec((1, share // 2, total), lambda r, order, odd: (order[r], 0, 0))
            ]
            * 2,
        ),
        compiler_params=pltpu.CompilerParams(vmem_limit_bytes=VMEM_LIMIT),
        cost_estimate=cost("weight_grad"),
        name="weight_grad",
    )(order, odd, *args, *after)


def place_blocks_kernel(order, value, out, turned):
    for r in range(4):
        out[r] = value[order[r]]
    rows = out.shape[0] * out.shape[1]
    turned[...] = out[...].reshape(rows, out.shape[2]).T


def place_blocks(value, t, after=()):
    rows, hidden = value.shape
    order = jnp.stack([t ^ m for m in (0, 2, 1, 3)]).astype(jnp.int32)
    placed, turned = run(
        place_blocks_kernel,
        [shaped(4, rows // 4, hidden), shaped(hidden, rows)],
        [order, value.reshape(4, rows // 4, hidden)],
        "place",
        10**6,
        scalars=1,
        after=after,
    )
    return placed.reshape(rows, hidden), turned


def gate(values, after):
    values, after = list(values), list(after)
    left = pl.BlockSpec(memory_space=pl.ANY)
    return pl.pallas_call(
        lambda *refs: None,
        out_shape=[jax.ShapeDtypeStruct(v.shape, v.dtype) for v in values],
        in_specs=[left] * (len(values) + len(after)),
        out_specs=[left] * len(values),
        input_output_aliases={i: i for i in range(len(values))},
        cost_estimate=pl.CostEstimate(flops=0, bytes_accessed=0, transcendentals=0),
        name="gate",
    )(*values, *after)


def dp_swap(value, mask):
    size = lax.axis_size("dp")
    return lax.ppermute(value, "dp", [(i, i ^ mask) for i in range(size)])


def gather_dp_whole(shard, t):
    size = lax.axis_size("dp")
    value = lax.all_gather(shard, "dp", axis=0, tiled=True)
    if size != 8:
        value = rel_blocks(value, t)
        return value, value.T
    return place_blocks(value, t)


def gather_first(shard):
    return [shard, *[dp_swap(shard, m) for m in (2, 4, 6)]]


def shard_order(t):
    pos = []
    for m in range(8):
        k = lax.axis_index("dp") ^ m
        b = t ^ (k >> 1)
        pos.append((((b & 1) << 1) | (b >> 1)) * 2 + (k & 1))
    return jnp.stack(pos).astype(jnp.int32)


def gather_second(near, far, t):
    return place(near, far, shard_order(t))


def gather_pair(near, far, cut, t):
    return place_pair(near, far, cut, shard_order(t))


def weight_whole(a, b, t, after=()):
    order = jnp.stack([t ^ m for m in (0, 2, 1, 3)]).astype(jnp.int32)
    return weight_grad(a, b, order, after)


def scatter_rows(value):
    return lax.psum_scatter(value, "dp", scatter_dimension=0, tiled=True).astype(F32)


def scatter_whole(a, b, t, after=()):
    return scatter_rows(weight_whole(a, b, t, after))


def scatter_split(groups, t, after=()):
    order = jnp.stack([t ^ m for m in (0, 2, 1, 3)]).astype(jnp.int32)
    me = lax.axis_index("dp")
    return weight_split(groups, order ^ (me >> 1), (me & 1).reshape(1).astype(jnp.int32), after)


def scatter_first(keep, came):
    total = keep + came.astype(F32)
    return total[0], [total[j].astype(LOW) for j in (1, 2, 3)]


def scatter_second(sends):
    return [dp_swap(send, 2 * j) for j, send in zip((1, 2, 3), sends)]


def scatter_last(own, came):
    return own + came[0].astype(F32) + came[1].astype(F32) + came[2].astype(F32)


def sum_dp(value):
    size = lax.axis_size("dp")
    if size != 8:
        return lax.psum(value, "dp")
    value = value + dp_swap(value, 1)
    return sum((dp_swap(value, m) for m in (2, 4, 6)), value)


def columns(vectors, count=8):
    vectors = [*vectors, *[jnp.zeros_like(vectors[0])] * (count - len(vectors))]
    return jnp.stack(vectors, axis=1)


def local(
    images,
    image_count,
    attn_gain,
    attn_shift,
    query_weight,
    query_bias,
    key_weight,
    value_weight,
    value_bias,
    output_weight,
    output_bias,
    mlp_gain,
    mlp_shift,
    up_weight,
    up_bias,
    down_weight,
    down_bias,
    cotangent,
):
    images, cotangent = images.transpose(0, 2, 1), cotangent.transpose(0, 2, 1)
    slots, share, seq = images.shape
    t = lax.axis_index("tensor")
    count = -(-seq // TILE) * TILE
    zero = jnp.zeros_like(output_bias)
    gains = [rel_blocks(a, t) for a in (attn_gain, attn_shift, mlp_gain, mlp_shift)]
    down_rows = jnp.concatenate([down_bias, zero, zero, zero])
    vec = columns([gains[0], gains[1], gains[1], gains[2], gains[3], down_rows])
    vec_own = vec[:share]
    qkv_bias = columns([jnp.concatenate([query_bias, zero, value_bias])])
    up_b = columns([up_bias])
    live = (jnp.arange(slots) < image_count[0]).astype(F32)

    fast = lax.axis_size("dp") == 8
    qkv_shard = jnp.concatenate([query_weight, key_weight, value_weight], axis=1)
    out_t = output_weight.T
    out_shard = jnp.concatenate([out_t, y_swap(out_t)], axis=1)
    up_value = lax.all_gather(up_weight, "dp", axis=0, tiled=True)
    x_own = prepare(images, columns([output_bias]), count)
    x_send, qkv_shard = gate([x_own, qkv_shard], [out_shard])
    x_far, x_across = core_swap(x_send), y_swap(x_send)
    if fast:
        near = gather_first(qkv_shard)
        cot_own, cot_sums = prepare_grad(cotangent, live, count, [x_own])
        out_shard = jnp.concatenate([out_shard, down_weight.T], axis=1)
        *near[1:], out_shard = gate([*near[1:], out_shard], [x_far, cot_sums])
        near_stack = jnp.stack(near)
        far = dp_swap(near_stack, 1)
        out_near = gather_first(out_shard)
        (x_across,) = gate([x_across], [near_stack])
        x_wide = core_swap(x_across)
        (cot_send,) = gate([cot_own], [x_wide])
        cot_across = y_swap(cot_send)
        qkv_w, qkv_t = gather_second(near, far, t)
    else:
        x_wide = core_swap(x_across)
        cot_own, cot_sums = prepare_grad(cotangent, live, count, [x_own])
        cot_across = y_swap(cot_own)
        qkv_w, qkv_t = gather_dp_whole(qkv_shard, t)
        o_half, _ = gather_dp_whole(out_shard, t)
        down_t, down_w = gather_dp_whole(down_weight.T, t)
        up_w, up_t = gather_dp_whole(up_weight, t)
    x = [x_own, x_across, x_far, x_wide]

    def forward(i, after):
        fwd.append(attn_fwd(x, i, vec, qkv_t, qkv_bias, seq, after))
        mixes.append([fwd[i][2], y_swap(fwd[i][2])])

    def widen(i):
        mixes[i].extend([core_swap(mixes[i][0]), core_swap(mixes[i][1])])

    fwd, mixes = [], []
    forward(0, [cot_sums])
    if fast:
        out_near[1:] = gate(out_near[1:], [fwd[0][4]])
        out_stack = jnp.stack(out_near)
        out_far = dp_swap(out_stack, 1)
        forward(1, [fwd[0][4], out_stack])
    else:
        forward(1, [fwd[0][4]])
    (cot_across,) = gate([cot_across], [fwd[1][4]])
    cot_far, cot_wide = core_swap(cot_own), core_swap(cot_across)
    forward(2, [fwd[1][4], cot_far])
    mixes[0][1], mixes[1][1] = gate([mixes[0][1], mixes[1][1]], [fwd[2][4], cot_wide])
    widen(0)
    widen(1)
    if fast:
        up_w, up_t = place_blocks(up_value, t, [cot_far, cot_wide])
    widen(2)
    if fast:
        (out_far,) = gate([out_far], [v for m in mixes for v in m])
        o_half, down_t, down_w = gather_pair(out_near, out_far, 2 * share, t)
    o_full, o_mine = join(o_half, core_swap(o_half))
    cot = [cot_own, cot_across, cot_far, cot_wide]

    mlp, back, ends, norm2_grad = [], [], [], []

    def mlp_forward(i, after):
        buffers = {j: mlp[i - 1][j] for j in (4, 6, 7)} if i else {}
        mlp.append(mlp_fwd(x, mixes[i], i, vec, o_full, up_t, up_b, down_t, seq, buffers, after))

    def mlp_back(i, after):
        back.append(mlp_bwd(cot, i, mlp[i][3], down_w, up_w, after))
        half = back[i][2] + core_swap(back[i][3]).astype(F32)
        send = half[::-1].astype(LOW)
        norm2_grad.append([half, y_swap(send)])
        return send

    def norm2_wide(i):
        half, across = norm2_grad[i]
        both = (half + across.astype(F32)).astype(LOW)
        norm2_grad[i].append(core_swap(both))
        return both

    def attention_back(i, after):
        attn_in, qkv, _, stats1, lse = fwd[i]
        norm2, stats2 = mlp[i][1], mlp[i][5]
        ends.append(
            attn_bwd(
                norm2_grad[i], back[i][0], norm2, stats2, vec, o_mine, qkv, lse, qkv_w, attn_in,
                seq, after,
            )
        )

    mlp_forward(0, [])
    send = mlp_back(0, [mlp[0][5]])
    mlp_forward(1, [send])
    norm2_grad[0][1], *_ = gate([norm2_grad[0][1]], [mlp[1][5]])
    both = norm2_wide(0)
    send = mlp_back(1, [both])
    mlp_forward(2, [send, norm2_grad[0][2]])
    norm2_grad[1][1], mlp_send = gate([norm2_grad[1][1], mlp[2][7]], [mlp[2][5]])
    both = norm2_wide(1)
    mlp_came = core_swap(mlp_send)
    send = mlp_back(2, [both])
    base, keep = mlp[2][4], mlp[2][6]
    (mlp_came,) = gate([mlp_came], [send])
    out_send = (keep + mlp_came[:, 1].astype(F32)).astype(LOW)

    up_rows = weight_whole(
        [m[0] for m in mlp], [b[1] for b in back], t, [send, norm2_grad[1][2], out_send]
    )
    up_grad = scatter_rows(up_rows)
    terms = [b[0] for b in back], [m[2] for m in mlp]
    if fast:
        down_keep, last = scatter_split([(*terms, None)], t, [up_rows])
        down_x = dp_swap(last, 1)
    else:
        last = weight_whole(*terms, t, [up_rows])
        down_grad = scatter_rows(last)
    norm2_grad[2][1], out_send = gate([norm2_grad[2][1], out_send], [last])
    both = norm2_wide(2)
    (out_send,) = gate([out_send], [both])
    out_across = y_swap(out_send)
    attention_back(0, [both, last])
    came = [core_swap(ends[0][5])]
    attention_back(1, [ends[0][-1], norm2_grad[2][2]])
    if fast:
        (down_x,) = gate([down_x], [ends[1][-1]])
        down_own, down_sends = scatter_first(down_keep, down_x)
        down_came = scatter_second(down_sends)
    came.append(core_swap(*gate([ends[1][5]], [came[0], out_across])))
    send = jnp.stack([(ends[i][4] + came[i][1].astype(F32)).astype(LOW) for i in (0, 1)])
    across = [y_swap(send)]
    qkv_part = weight_part([f[0] for f in fwd[:2]], [e[2] for e in ends], [send])
    out_part = weight_part([e[0] for e in ends], [f[2] for f in fwd[:2]], [send])
    attention_back(2, [qkv_part, out_part, up_grad])
    e = ends[2]
    stats = jnp.concatenate([v[6] for v in ends])
    if fast:
        keep_a, send_a = scatter_split([([fwd[2][0]], [e[2]], qkv_part)], t, [e[-1]])
        x_a = dp_swap(send_a, 1)
        part, stats, *down_came = gate([e[5], stats, *down_came], [send_a])
        down_grad = scatter_last(down_own, down_came)
    else:
        qkv_grad = scatter_whole([f[0] for f in fwd], [v[2] for v in ends], t)
        out_grad = scatter_whole([v[0] for v in ends], [f[2] for f in fwd], t)
        part = e[5]
    came_last = core_swap(part)
    came.append(came_last)
    send = (e[4] + came_last[1].astype(F32)).astype(LOW)[None]
    stats = stats + core_swap(stats)
    across.append(y_swap(send))
    stats = stats + y_swap(stats)
    if fast:
        keep_b, send_b = scatter_split([([e[0]], [fwd[2][2]], out_part)], t, [send])
        x_b = dp_swap(send_b, 1)
        (out_across,) = gate([out_across], [send_b])
        own_a, sends_a = scatter_first(keep_a, x_a)
        came_a = scatter_second(sends_a)
    out_buffer = finish_out(live, base, mlp_came, out_across, seq)
    grad_buffer, sums = None, None
    for i in range(slots):
        grad_buffer, grad_sums = finish_grad(
            [ends[i][1], ends[i][3], came[i], (across[i // 2], i % 2), (x_own, i), fwd[i][3],
             stats[8 * i : 8 * i + 8], vec_own],
            i, grad_buffer, slots, seq,
        )
        now = (grad_sums, ends[i][7], ends[i][8], back[i][-1])
        sums = now if sums is None else jax.tree.map(jnp.add, sums, now)
    if fast:
        *came_a, x_b = gate([*came_a, x_b], [send_b, grad_sums])
        own_b, sends_b = scatter_first(keep_b, x_b)
        came_b = scatter_second(sends_b)
        qkv_grad = scatter_last(own_a, came_a)
        out_grad = scatter_last(own_b, came_b)
    down_grad, out_grad = down_grad.T, out_grad.T
    sums = (*sums, cot_sums)
    sizes = [2 * share, 3 * share, 3 * share, up_bias.shape[0], share]
    small = jnp.concatenate(
        [
            sums[0][:, :2].T.reshape(-1),
            sums[1][:, :3].T.reshape(-1),
            sums[2][0],
            sums[3][0],
            sums[4][0],
        ]
    )
    if fast:
        (small,) = gate([small], [x_b])
    small = sum_dp(small)
    parts, at = [], 0
    for size in sizes:
        parts.append(small[at : at + size])
        at += size
    grad_sums, own_sums = parts[0].reshape(2, share), parts[1].reshape(3, share)
    qkv_sums, up_sum, cot_sum = parts[2:]
    return (
        out_buffer.transpose(0, 2, 1),
        grad_buffer.transpose(0, 2, 1),
        grad_sums[0],
        grad_sums[1],
        qkv_grad[:, :share],
        qkv_sums[:share],
        qkv_grad[:, share : 2 * share],
        qkv_grad[:, 2 * share :],
        qkv_sums[2 * share :],
        out_grad,
        own_sums[0],
        own_sums[1],
        own_sums[2],
        up_grad,
        up_sum,
        down_grad,
        cot_sum,
    )


def solution(mesh):
    in_specs = (
        P("dp", None, "tensor"),
        P("dp"),
        P(),
        P(),
        P("dp", "tensor"),
        P("tensor"),
        P("dp", "tensor"),
        P("dp", "tensor"),
        P("tensor"),
        P("tensor", "dp"),
        P("tensor"),
        P(),
        P(),
        P("dp", "tensor"),
        P("tensor"),
        P("tensor", "dp"),
        P("tensor"),
        P("dp", None, "tensor"),
    )
    out_specs = (
        P("dp", None, "tensor"),
        P("dp", None, "tensor"),
        P("tensor"),
        P("tensor"),
        P("dp", "tensor"),
        P("tensor"),
        P("dp", "tensor"),
        P("dp", "tensor"),
        P("tensor"),
        P("tensor", "dp"),
        P("tensor"),
        P("tensor"),
        P("tensor"),
        P("dp", "tensor"),
        P("tensor"),
        P("tensor", "dp"),
        P("tensor"),
    )
    return jax.shard_map(local, mesh=mesh, in_specs=in_specs, out_specs=out_specs, check_vma=False)
```
